32 devices in a mesh: ctx: 16 (over z, y, x), tp: 2 (over core).
Axes of the slice: x: 2, y: 2, z: 4, core: 2. Of those that a mesh axis runs over, the one named last changes fastest.
Arguments:
- outer_input: bfloat16 [1024, 8192], P('ctx', 'tp'), may hold values from -6 to 6
- inner_input: bfloat16 [1024, 8192], P('ctx', 'tp'), may hold values from -6 to 6
- value_input: bfloat16 [1024, 8192], P('ctx', 'tp'), may hold values from -6 to 6
- feature_taps: bfloat16 [3, 7, 8192], P(None, None, 'tp'), may hold values from -2 to 2
- medium_taps: bfloat16 [128, 512], P(None, 'tp'), may hold values from -0.5 to 0.5
- decay_rates: float32 [512, 16], P('tp'), may hold values from 1e-05 to 0.04
- residues: float32 [512, 16], P('tp'), may hold values from -4 to 4
- residual: bfloat16 [1024, 8192], P('ctx', 'tp'), may hold values from -72 to 72
- norm_gain: bfloat16 [8192], P('tp'), may hold values from 0.5 to 1.5
Outputs:
- normed: bfloat16 [1024, 8192], P('ctx', 'tp')
The draws below stay inside these ranges and needn't reach their ends.
All inputs are finite; a program needn't handle non-finite values.
Results may differ from the reference program's by a relative error of at most 0.0039.
Values may be sent and summed in bfloat16 or wider, within the bound.
A program may use at most 128 MiB of HBM per device.

```python
import math
import jax
import jax.numpy as jnp
from jax import lax

D = 8192
GROUP = 16
MODES = 16
FEAT_TAPS = 7
MR_TAPS = 128
SEQ = 1024
GROUPS = 512


def draw_decay_rates(key, part):
    key_slow = jax.random.fold_in(jax.random.fold_in(key, 31), 0)
    log_low = math.log(1e-05)
    rates = jnp.exp(jax.random.uniform(key_slow, (GROUPS, MODES), minval=log_low, maxval=math.log(0.04)))
    return jnp.clip(rates, 1e-05, 0.04).astype(jnp.float32)


def draw_residual(key, part):
    key_base, key_column, key_row = jax.random.split(jax.random.fold_in(key, 41), 3)
    channel = jnp.arange(D, dtype=jnp.float32)
    ramp = jnp.sqrt(1.0 + 3.0 * channel / D)[None, :]
    column_scale = jnp.exp(jax.random.uniform(key_column, (1, D), minval=math.log(0.3), maxval=math.log(3.0)))
    row_scale = jnp.exp(jax.random.uniform(key_row, (SEQ, 1), minval=math.log(0.3), maxval=math.log(3.0)))
    base = jnp.clip(jax.random.normal(key_base, (SEQ, D)), -4.0, 4.0)
    return (base * row_scale * column_scale * ramp).astype(jnp.bfloat16)


def shard_levels(rng, extent, shards, least, largest):
    gain = 1.0
    for position, parts in shards:
        steps = jax.random.uniform(jax.random.fold_in(jax.random.fold_in(rng, 6), position), (parts,), jnp.float32, least / len(shards), largest / len(shards))
        gain = gain * jnp.repeat(jnp.exp(steps), extent[position] // parts).reshape((-1,) + (1,) * (len(extent) - 1 - position))
    return gain


def gaussian(key, extent, width, limit, cuts=(), kind=jnp.bfloat16):
    values = width * jax.random.normal(key, extent, jnp.float32)
    if cuts:
        values = values * shard_levels(key, extent, cuts, -0.22, 0.18)
    return jnp.clip(values, -limit, limit).astype(kind)


def setup_inputs(seed: int = 0) -> dict:
    streams_of = jax.random.split(jax.random.key(seed), 10)
    return {
        "outer_input": gaussian(streams_of[0], (SEQ, D), 1.0, 6.0, ((0, 16), (1, 2))),
        "inner_input": gaussian(streams_of[1], (SEQ, D), 1.0, 6.0, ((0, 16), (1, 2))),
        "value_input": gaussian(streams_of[2], (SEQ, D), 1.0, 6.0, ((0, 16), (1, 2))),
        "feature_taps": gaussian(streams_of[3], (3, FEAT_TAPS, D), FEAT_TAPS ** -0.5, 2.0, ((2, 2),)),
        "medium_taps": gaussian(streams_of[4], (MR_TAPS, GROUPS), MR_TAPS ** -0.5, 0.5, ((1, 2),)),
        "decay_rates": draw_decay_rates(jax.random.fold_in(streams_of[9], 71), 0),
        "residues": gaussian(streams_of[6], (GROUPS, MODES), 1.0, 4.0, ((0, 2),), jnp.float32),
        "residual": draw_residual(jax.random.fold_in(streams_of[9], 71), 0),
        "norm_gain": jnp.clip(1.0 + 0.1 * jax.random.normal(streams_of[8], (D,), jnp.float32), 0.5, 1.5).astype(jnp.bfloat16),
    }


def featurize(signal, tap_table):
    seq_rows = signal.shape[0]
    rim_rows = tap_table.shape[0] - 1
    padded = jnp.pad(signal.astype(jnp.float32), ((rim_rows, 0), (0, 0)))
    summed = jnp.zeros(signal.shape, jnp.float32)
    for offset in range(tap_table.shape[0]):
        window = padded[rim_rows - offset:rim_rows - offset + seq_rows]
        summed = summed + tap_table[offset].astype(jnp.float32)[None, :] * window
    return summed

def causal_conv(product, filters):
    seq_rows = product.shape[0]
    fft_length = 2 * seq_rows
    step_groups = max(1, GROUPS // 8)
    outputs = []
    for group_start in range(0, GROUPS, step_groups):
        group_end = min(GROUPS, group_start + step_groups)
        channel_block = product[:, group_start * GROUP:group_end * GROUP].astype(jnp.float32)
        spectrum = jnp.fft.rfft(channel_block, n=fft_length, axis=0)
        kernel = jnp.fft.rfft(filters[:, group_start:group_end], n=fft_length, axis=0)
        kernel = jnp.repeat(kernel, GROUP, axis=1)
        result = jnp.fft.irfft(spectrum * kernel, n=fft_length, axis=0)[:seq_rows]
        outputs.append(result.astype(jnp.float32))
    return jnp.concatenate(outputs, 1)

def reference(outer_input, inner_input, value_input, feature_taps, medium_taps, decay_rates, residues, residual, norm_gain):
    seq_rows = outer_input.shape[0]
    outer_feat = featurize(outer_input, feature_taps[0])
    inner_feat = featurize(inner_input, feature_taps[1])
    value_feat = featurize(value_input, feature_taps[2])
    product = (inner_feat * value_feat).astype(jnp.bfloat16)
    lag_rows = jnp.arange(seq_rows, dtype=jnp.int32).astype(jnp.float32)[:, None]
    mode_weight = residues * jnp.sqrt(2.0 * decay_rates / MODES)
    long_filter = jnp.zeros((seq_rows, GROUPS), jnp.float32)
    for mode_index in range(MODES):
        long_filter = long_filter + mode_weight[:, mode_index][None, :] * jnp.exp(-decay_rates[:, mode_index][None, :] * lag_rows)
    filters = long_filter.at[:MR_TAPS].add(medium_taps.astype(jnp.float32))
    mixed_conv = causal_conv(product, filters)
    hidden = residual.astype(jnp.float32) + outer_feat * mixed_conv
    square_sum = lax.optimization_barrier(jnp.sum(hidden * hidden, axis=1, keepdims=True))
    normed = (hidden * norm_gain.astype(jnp.float32)[None, :] / jnp.sqrt(square_sum / D + 1e-05)).astype(jnp.bfloat16)
    return normed
```

```python
import functools
import jax
import jax.numpy as jnp
from jax import lax
from jax.experimental import pallas as pl
from jax.experimental.pallas import tpu as pltpu
from jax.sharding import PartitionSpec as P

MESH = pl.DeviceIdType.MESH
BLOCK = 128

D = 8192


def passed_along(array, axis, by):
    size = lax.axis_size(axis)
    pairs = [(i, i + by) for i in range(size) if 0 <= i + by < size]
    return lax.ppermute(array, axis, pairs)


def entering(part, axis, combine, identity):
    place = lax.axis_index(axis)
    gathered = jax.tree.map(lambda a: lax.all_gather(a, axis), part)
    state = jax.tree.map(lambda a, e: jnp.zeros_like(a) + jnp.asarray(e, a.dtype), part, identity)

    def one(lap, state):
        return combine(
            state, jax.tree.map(lambda a: lax.dynamic_index_in_dim(a, lap, 0, False), gathered)
        )

    return lax.fori_loop(0, place, one, state)


def banded(reversed_taps, row_count, width):
    group_count, tap_count = reversed_taps.shape
    period = width + 1
    padded = jnp.pad(reversed_taps, ((0, 0), (0, period - tap_count)))
    tiled = jnp.tile(padded, (1, row_count))
    return tiled[:, : row_count * width].reshape(group_count, row_count, width)


def featurize(extended, tap_table, row_count):
    rim_rows = tap_table.shape[0] - 1
    summed = jnp.zeros((row_count, extended.shape[1]), jnp.float32)
    for offset in range(tap_table.shape[0]):
        window = extended[rim_rows - offset : rim_rows - offset + row_count].astype(jnp.float32)
        summed = summed + tap_table[offset].astype(jnp.float32)[None, :] * window
    return summed


def product_rim(product, rim_depth):
    row_count = product.shape[0]
    pieces = []
    for distance in range(1, (rim_depth - 1) // row_count + 2):
        needed = min(row_count, rim_depth - (distance - 1) * row_count)
        arrived = passed_along(product[row_count - needed :], "ctx", distance)
        pieces = [arrived] + pieces
    return jnp.concatenate(pieces, 0)


def combine_modes(earlier, later):
    return (earlier[0] * later[0], earlier[1] * later[0] + later[1])


def plain(
    outer_input,
    inner_input,
    value_input,
    feature_taps,
    medium_taps,
    decay_rates,
    residues,
    residual,
    norm_gain,
):
    row_count, channels = outer_input.shape
    group_count, mode_count = decay_rates.shape
    group_width = channels // group_count
    feat_rim = feature_taps.shape[1] - 1
    medium_rim = medium_taps.shape[0] - 1
    highest = lax.Precision.HIGHEST
    rim_outer, rim_inner, rim_value = passed_along(
        (
            outer_input[row_count - feat_rim :],
            inner_input[row_count - feat_rim :],
            value_input[row_count - feat_rim :],
        ),
        "ctx",
        1,
    )
    inner_feat = featurize(jnp.concatenate([rim_inner, inner_input], 0), feature_taps[1], row_count)
    value_feat = featurize(jnp.concatenate([rim_value, value_input], 0), feature_taps[2], row_count)
    product = (inner_feat * value_feat).astype(jnp.bfloat16)
    extended = jnp.concatenate([product_rim(product, medium_rim), product], 0)
    outer_feat = featurize(jnp.concatenate([rim_outer, outer_input], 0), feature_taps[0], row_count)
    band_medium = banded(medium_taps[::-1].T, row_count, row_count + medium_rim)
    extended_groups = extended.reshape(row_count + medium_rim, group_count, group_width)
    medium_part = jnp.einsum(
        "gts,sgc->tgc", band_medium, extended_groups, preferred_element_type=jnp.float32
    )
    lag_rows = jnp.arange(row_count, dtype=jnp.float32)[:, None, None]
    mode_weight = residues * jnp.sqrt(2.0 * decay_rates / mode_count)
    powers = jnp.exp(-decay_rates[None] * lag_rows)
    long_taps = jnp.sum(powers * mode_weight[None], axis=2)
    band_long = banded(long_taps[::-1].T, row_count, 2 * row_count - 1)[:, :, row_count - 1 :]
    product_wide = product.reshape(row_count, group_count, group_width).astype(jnp.float32)
    within = jnp.einsum("gts,sgc->tgc", band_long, product_wide, precision=highest)
    to_end = jnp.exp(-decay_rates[None] * (row_count - 1.0 - lag_rows))
    local_state = jnp.einsum("tgc,tgn->gcn", product_wide, to_end, precision=highest)
    block_decay = jnp.exp(-decay_rates * row_count)[:, None, :]
    neutral = (jnp.ones_like(block_decay), jnp.zeros_like(local_state))
    prefix = entering((block_decay, local_state), "ctx", combine_modes, neutral)
    incoming = prefix[1]
    from_start = powers * jnp.exp(-decay_rates)[None]
    carried = jnp.einsum(
        "tgn,gcn->tgc", from_start, incoming * mode_weight[:, None, :], precision=highest
    )
    mixed_conv = (medium_part + within + carried).reshape(row_count, channels)
    hidden = residual.astype(jnp.float32) + outer_feat * mixed_conv
    square_sum = lax.psum(jnp.sum(hidden * hidden, axis=1), "tp")
    normed = (
        hidden * norm_gain.astype(jnp.float32)[None, :] / jnp.sqrt(square_sum / D + 1e-05)[:, None]
    ).astype(jnp.bfloat16)
    return normed


def fused_kernel(
    n,
    tpn,
    outer_ref,
    inner_ref,
    value_ref,
    taps_ref,
    medium_ref,
    decay_ref,
    residues_ref,
    residual_ref,
    gain_ref,
    out_ref,
    halo_out,
    halo_in,
    gate_out,
    gate_in,
    ext_a,
    ext_b,
    prod_out,
    prod_all,
    medium_rev,
    filt_rev,
    toep,
    mixed_out,
    mixed_in,
    hidden,
    sq_out,
    sq_in,
    halo_send,
    halo_recv,
    prod_send,
    prod_recv,
    mixed_send,
    mixed_recv,
    sq_send,
    sq_recv,
):
    f32 = jnp.float32
    me = lax.axis_index("ctx")
    tp_me = lax.axis_index("tp")
    rows, channels = outer_ref.shape
    width = channels // n
    mode_count = decay_ref.shape[1]
    group_width = channels // decay_ref.shape[0]
    group_count = width // group_width
    tap_count = taps_ref.shape[1]
    block_count = n * rows // BLOCK
    per_block = BLOCK // rows
    tile_groups = 128 // group_width
    half = channels // 2

    barrier = pltpu.get_barrier_semaphore()

    def greet(k, carry):
        pl.semaphore_signal(
            barrier, inc=1, device_id={"ctx": lax.rem(me + k, n)}, device_id_type=MESH
        )
        return carry

    lax.fori_loop(1, n, greet, 0)
    for k in range(1, tpn):
        pl.semaphore_signal(
            barrier, inc=1, device_id={"tp": lax.rem(tp_me + k, tpn)}, device_id_type=MESH
        )

    def last_rows(ref, start, size):
        return ref[rows - 16 : rows, pl.ds(start, size)].astype(f32)[8:16]

    for start in range(0, channels, 512):
        halo_out[:, pl.ds(start, 512)] = jnp.concatenate(
            [last_rows(inner_ref, start, 512), last_rows(value_ref, start, 512)], 0
        ).astype(jnp.bfloat16)
    for start in range(0, half, 512):
        gate_out[:, pl.ds(start, 512)] = jnp.concatenate(
            [last_rows(outer_ref, start, 512), last_rows(outer_ref, half + start, 512)], 0
        ).astype(jnp.bfloat16)

    pl.semaphore_wait(barrier, n - 1 + tpn - 1)

    def halo_copy(src, dst, index):
        return pltpu.make_async_remote_copy(
            src_ref=src,
            dst_ref=dst,
            send_sem=halo_send.at[index],
            recv_sem=halo_recv.at[index],
            device_id={"ctx": lax.rem(me + 1, n)},
            device_id_type=MESH,
        )

    halo_copies = [halo_copy(halo_out, halo_in, 0), halo_copy(gate_out, gate_in, 1)]

    @pl.when(me < n - 1)
    def _():
        for copy in halo_copies:
            copy.start()

    @pl.when(me == 0)
    def _():
        halo_in[...] = jnp.zeros_like(halo_in)
        gate_in[...] = jnp.zeros_like(gate_in)

    tap_index = lax.broadcasted_iota(jnp.int32, (BLOCK, BLOCK), 0)
    lane_index = lax.broadcasted_iota(jnp.int32, (BLOCK, BLOCK), 1)
    for m in range(2):
        pick = jnp.where(tap_index == BLOCK * m - lane_index, 1.0, 0.0).astype(jnp.bfloat16)
        medium_rev[m] = lax.dot_general(
            medium_ref[...], pick, (((0,), (0,)), ((), ())), preferred_element_type=f32
        )
    own_groups = pl.ds(pl.multiple_of(me * group_count, group_count), group_count)
    decay = decay_ref[own_groups, :]
    weight = residues_ref[own_groups, :] * jnp.sqrt(2.0 * decay / mode_count)
    lanes = lax.broadcasted_iota(jnp.int32, (group_count, BLOCK), 1)
    for m in range(block_count + 1):
        lag = BLOCK * m - lanes
        lag_rows = jnp.maximum(lag, 0).astype(f32)
        total = jnp.zeros((group_count, BLOCK), f32)
        for mode in range(mode_count):
            total = total + weight[:, mode : mode + 1] * jnp.exp(
                -decay[:, mode : mode + 1] * lag_rows
            )
        total = jnp.where(lag >= 0, total, 0.0)
        if m < 2:
            total = total + medium_rev[m, own_groups, :]
        filt_rev[m] = total

    def featurize(which, ref, rim, ext, start, size):
        ext[0:8, :] = rim
        ext[8 : 8 + rows, :] = ref[:, pl.ds(start, size)].astype(f32)
        taps = taps_ref[which, :, pl.ds(start, size)].astype(f32)
        summed = taps[0:1] * ext[8 : 8 + rows, :]
        for offset in range(1, tap_count):
            summed = summed + taps[offset : offset + 1] * ext[8 - offset : 8 - offset + rows, :]
        return summed

    def product_for(owner):
        start = pl.multiple_of(owner * width, width)
        rim = halo_in[:, pl.ds(start, width)].astype(f32)
        inner_feat = featurize(1, inner_ref, rim[0:8], ext_a, start, width)
        value_feat = featurize(2, value_ref, rim[8:16], ext_b, start, width)
        return (inner_feat * value_feat).astype(jnp.bfloat16)

    def own_rows(place):
        return pl.ds(pl.multiple_of(place * rows, rows), rows)

    def product_copy(k):
        return pltpu.make_async_remote_copy(
            src_ref=prod_out.at[k],
            dst_ref=prod_all.at[own_rows(me)],
            send_sem=prod_send.at[k],
            recv_sem=prod_recv.at[k],
            device_id={"ctx": lax.rem(me + k, n)},
            device_id_type=MESH,
        )

    @pl.when(me > 0)
    def _():
        for copy in halo_copies:
            copy.wait_recv()

    def send_product(k, carry):
        prod_out[k] = product_for(lax.rem(me + k, n))
        product_copy(k).start()
        return carry

    lax.fori_loop(1, n, send_product, 0)
    prod_all[own_rows(me), :] = product_for(me)

    def gate_chunk(chunk, carry):
        start = pl.multiple_of(chunk * width, width)
        low = chunk < n // 2
        rim_start = pl.multiple_of(lax.rem(chunk, n // 2) * width, width)
        rim = gate_in[:, pl.ds(rim_start, width)].astype(f32)
        rim = jnp.where(low, rim[0:8], rim[8:16])
        hidden[:, pl.ds(start, width)] = featurize(0, outer_ref, rim, ext_a, start, width)
        return carry

    lax.fori_loop(0, n, gate_chunk, 0)

    def build(g, carry):
        block_rows = pl.ds(pl.multiple_of(g * BLOCK, BLOCK), BLOCK)
        upper = lane_index >= tap_index
        earlier = None
        for m in range(block_count + 1):
            row = jnp.broadcast_to(filt_rev[m, pl.ds(g, 1), :], (BLOCK, BLOCK))
            rolled = pltpu.roll(row, 0, 1, stride=1, stride_axis=0)
            if m > 0:
                place = (block_count - m) * BLOCK
                toep[block_rows, place : place + BLOCK] = jnp.where(
                    upper, earlier, rolled
                ).astype(jnp.bfloat16)
            earlier = rolled
        return carry

    lax.fori_loop(0, group_count, build, 0)

    def mixed_copy(place):
        return pltpu.make_async_remote_copy(
            src_ref=mixed_out.at[place],
            dst_ref=mixed_in.at[me],
            send_sem=mixed_send.at[place],
            recv_sem=mixed_recv.at[lax.rem(place - me + n, n)],
            device_id={"ctx": place},
            device_id_type=MESH,
        )

    lane_group = lax.broadcasted_iota(jnp.int32, (BLOCK, 128), 1) // group_width
    for block in range(block_count):
        for place in range(block * per_block, (block + 1) * per_block):

            @pl.when(me != place)
            def _():
                pltpu.make_async_remote_copy(
                    src_ref=prod_out.at[0],
                    dst_ref=prod_all.at[place * rows : (place + 1) * rows],
                    send_sem=prod_send.at[0],
                    recv_sem=prod_recv.at[lax.rem(me - place + n, n)],
                    device_id={"ctx": place},
                    device_id_type=MESH,
                ).wait_recv()

        depth = (block + 1) * BLOCK
        first = (block_count - 1 - block) * BLOCK

        for tile in range(width // 128):
            source = prod_all[0:depth, tile * 128 : (tile + 1) * 128]
            mixed = jnp.zeros((BLOCK, 128), f32)
            for part in range(0, tile_groups, 4):
                base = (tile * tile_groups + part) * BLOCK
                sums = jnp.dot(
                    toep[base : base + 4 * BLOCK, first:],
                    source,
                    preferred_element_type=f32,
                )
                for g in range(4):
                    mixed = jnp.where(
                        lane_group == part + g, sums[g * BLOCK : (g + 1) * BLOCK], mixed
                    )
            mixed = mixed.astype(jnp.bfloat16)
            for which in range(per_block):
                mixed_out[block * per_block + which, :, tile * 128 : (tile + 1) * 128] = mixed[
                    which * rows : (which + 1) * rows
                ]

        for place in range(block * per_block, (block + 1) * per_block):

            @pl.when(me != place)
            def _():
                mixed_copy(place).start()

            @pl.when(me == place)
            def _():
                mixed_in[place] = mixed_out[place]

    def gather_hidden(k, square):
        source = lax.rem(me - k + n, n)

        @pl.when(k > 0)
        def _():
            pltpu.make_async_remote_copy(
                src_ref=mixed_out.at[0],
                dst_ref=mixed_in.at[source],
                send_sem=mixed_send.at[0],
                recv_sem=mixed_recv.at[k],
                device_id={"ctx": source},
                device_id_type=MESH,
            ).wait_recv()

        chunk = pl.ds(pl.multiple_of(source * width, width), width)
        value = residual_ref[:, chunk].astype(f32) + hidden[:, chunk] * mixed_in[source].astype(f32)
        hidden[:, chunk] = value
        for tile in range(width // 128):
            piece = value[:, tile * 128 : (tile + 1) * 128]
            square = square + piece * piece
        return square

    square = lax.fori_loop(0, n, gather_hidden, jnp.zeros((rows, 128), f32))
    sq_out[...] = square

    def square_copy(k):
        return pltpu.make_async_remote_copy(
            src_ref=sq_out,
            dst_ref=sq_in.at[k],
            send_sem=sq_send.at[k],
            recv_sem=sq_recv.at[k],
            device_id={"tp": lax.rem(tp_me + k, tpn)},
            device_id_type=MESH,
        )

    for k in range(1, tpn):
        square_copy(k).start()
    for k in range(1, tpn):
        square_copy(k).wait_recv()
        square = square + sq_in[k]
    square_sum = jnp.sum(square, axis=1, keepdims=True)
    scale = 1.0 / jnp.sqrt(square_sum / (channels * tpn) + 1e-05)

    def finish(chunk, carry):
        place = pl.ds(pl.multiple_of(chunk * width, width), width)
        gain = gain_ref[:, place].astype(f32)
        out_ref[:, place] = (hidden[:, place] * gain * scale).astype(jnp.bfloat16)
        return carry

    lax.fori_loop(0, n, finish, 0)

    @pl.when(me < n - 1)
    def _():
        for copy in halo_copies:
            copy.wait_send()

    def drain(k, carry):
        product_copy(k).wait_send()
        return carry

    lax.fori_loop(1, n, drain, 0)

    def drain_mixed(place, carry):
        @pl.when(me != place)
        def _():
            mixed_copy(place).wait_send()

        return carry

    lax.fori_loop(0, n, drain_mixed, 0)
    for k in range(1, tpn):
        square_copy(k).wait_send()


def fused(n, tpn, *args):
    outer_input, inner_input, value_input, taps, medium, decay, residues, residual, gain = args
    rows, channels = outer_input.shape
    width = channels // n
    group_count = decay.shape[0] // n
    seq = n * rows
    blocks = seq // BLOCK
    bf16, f32 = jnp.bfloat16, jnp.float32
    dma = pltpu.SemaphoreType.DMA
    return pl.pallas_call(
        functools.partial(fused_kernel, n, tpn),
        out_shape=jax.ShapeDtypeStruct((rows, channels), bf16),
        in_specs=[pl.BlockSpec(memory_space=pltpu.VMEM)] * 9,
        out_specs=pl.BlockSpec(memory_space=pltpu.VMEM),
        scratch_shapes=[
            pltpu.VMEM((16, channels), bf16),
            pltpu.VMEM((16, channels), bf16),
            pltpu.VMEM((16, channels // 2), bf16),
            pltpu.VMEM((16, channels // 2), bf16),
            pltpu.VMEM((rows + 8, width), f32),
            pltpu.VMEM((rows + 8, width), f32),
            pltpu.VMEM((n, rows, width), bf16),
            pltpu.VMEM((seq, width), bf16),
            pltpu.VMEM((2, decay.shape[0], BLOCK), f32),
            pltpu.VMEM((blocks + 1, group_count, BLOCK), f32),
            pltpu.VMEM((group_count * BLOCK, blocks * BLOCK), bf16),
            pltpu.VMEM((n, rows, width), bf16),
            pltpu.VMEM((n, rows, width), bf16),
            pltpu.VMEM((rows, channels), f32),
            pltpu.VMEM((rows, 128), f32),
            pltpu.VMEM((tpn, rows, 128), f32),
            dma((2,)),
            dma((2,)),
            dma((n,)),
            dma((n,)),
            dma((n,)),
            dma((n,)),
            dma((tpn,)),
            dma((tpn,)),
        ],
        compiler_params=pltpu.CompilerParams(
            collective_id=0, has_side_effects=True, vmem_limit_bytes=40 * 1024 * 1024
        ),
    )(outer_input, inner_input, value_input, taps, medium, decay, residues, residual, gain[None, :])


def on_device(*args):
    n, tpn = lax.axis_size("ctx"), lax.axis_size("tp")
    rows, channels = args[0].shape
    medium_rows = args[4].shape[0]
    groups = args[5].shape[0]
    fits = (
        channels % (n * 128) == 0
        and BLOCK % rows == 0
        and rows % 16 == 0
        and groups % (8 * n) == 0
        and medium_rows == BLOCK
    )
    if fits:
        return fused(n, tpn, *args)
    return plain(*args)


def solution(mesh):
    return jax.shard_map(
        on_device,
        mesh=mesh,
        in_specs=(
            P("ctx", "tp"),
            P("ctx", "tp"),
            P("ctx", "tp"),
            P(None, None, "tp"),
            P(None, "tp"),
            P("tp", None),
            P("tp", None),
            P("ctx", "tp"),
            P("tp"),
        ),
        out_specs=P("ctx", "tp"),
        check_vma=False,
    )
```

```python
import functools
import jax
import jax.numpy as jnp
from jax import lax
from jax.experimental import pallas as pl
from jax.experimental.pallas import tpu as pltpu
from jax.sharding import PartitionSpec as P

MESH = pl.DeviceIdType.MESH
BLOCK = 128

D = 8192


def passed_along(array, axis, by):
    size = lax.axis_size(axis)
    pairs = [(i, i + by) for i in range(size) if 0 <= i + by < size]
    return lax.ppermute(array, axis, pairs)


def entering(part, axis, combine, identity):
    place = lax.axis_index(axis)
    gathered = jax.tree.map(lambda a: lax.all_gather(a, axis), part)
    state = jax.tree.map(lambda a, e: jnp.zeros_like(a) + jnp.asarray(e, a.dtype), part, identity)

    def one(lap, state):
        return combine(
            state, jax.tree.map(lambda a: lax.dynamic_index_in_dim(a, lap, 0, False), gathered)
        )

    return lax.fori_loop(0, place, one, state)


def banded(reversed_taps, row_count, width):
    group_count, tap_count = reversed_taps.shape
    period = width + 1
    padded = jnp.pad(reversed_taps, ((0, 0), (0, period - tap_count)))
    tiled = jnp.tile(padded, (1, row_count))
    return tiled[:, : row_count * width].reshape(group_count, row_count, width)


def featurize(extended, tap_table, row_count):
    rim_rows = tap_table.shape[0] - 1
    summed = jnp.zeros((row_count, extended.shape[1]), jnp.float32)
    for offset in range(tap_table.shape[0]):
        window = extended[rim_rows - offset : rim_rows - offset + row_count].astype(jnp.float32)
        summed = summed + tap_table[offset].astype(jnp.float32)[None, :] * window
    return summed


def product_rim(product, rim_depth):
    row_count = product.shape[0]
    pieces = []
    for distance in range(1, (rim_depth - 1) // row_count + 2):
        needed = min(row_count, rim_depth - (distance - 1) * row_count)
        arrived = passed_along(product[row_count - needed :], "ctx", distance)
        pieces = [arrived] + pieces
    return jnp.concatenate(pieces, 0)


def combine_modes(earlier, later):
    return (earlier[0] * later[0], earlier[1] * later[0] + later[1])


def plain(
    outer_input,
    inner_input,
    value_input,
    feature_taps,
    medium_taps,
    decay_rates,
    residues,
    residual,
    norm_gain,
):
    row_count, channels = outer_input.shape
    group_count, mode_count = decay_rates.shape
    group_width = channels // group_count
    feat_rim = feature_taps.shape[1] - 1
    medium_rim = medium_taps.shape[0] - 1
    highest = lax.Precision.HIGHEST
    rim_outer, rim_inner, rim_value = passed_along(
        (
            outer_input[row_count - feat_rim :],
            inner_input[row_count - feat_rim :],
            value_input[row_count - feat_rim :],
        ),
        "ctx",
        1,
    )
    inner_feat = featurize(jnp.concatenate([rim_inner, inner_input], 0), feature_taps[1], row_count)
    value_feat = featurize(jnp.concatenate([rim_value, value_input], 0), feature_taps[2], row_count)
    product = (inner_feat * value_feat).astype(jnp.bfloat16)
    extended = jnp.concatenate([product_rim(product, medium_rim), product], 0)
    outer_feat = featurize(jnp.concatenate([rim_outer, outer_input], 0), feature_taps[0], row_count)
    band_medium = banded(medium_taps[::-1].T, row_count, row_count + medium_rim)
    extended_groups = extended.reshape(row_count + medium_rim, group_count, group_width)
    medium_part = jnp.einsum(
        "gts,sgc->tgc", band_medium, extended_groups, preferred_element_type=jnp.float32
    )
    lag_rows = jnp.arange(row_count, dtype=jnp.float32)[:, None, None]
    mode_weight = residues * jnp.sqrt(2.0 * decay_rates / mode_count)
    powers = jnp.exp(-decay_rates[None] * lag_rows)
    long_taps = jnp.sum(powers * mode_weight[None], axis=2)
    band_long = banded(long_taps[::-1].T, row_count, 2 * row_count - 1)[:, :, row_count - 1 :]
    product_wide = product.reshape(row_count, group_count, group_width).astype(jnp.float32)
    within = jnp.einsum("gts,sgc->tgc", band_long, product_wide, precision=highest)
    to_end = jnp.exp(-decay_rates[None] * (row_count - 1.0 - lag_rows))
    local_state = jnp.einsum("tgc,tgn->gcn", product_wide, to_end, precision=highest)
    block_decay = jnp.exp(-decay_rates * row_count)[:, None, :]
    neutral = (jnp.ones_like(block_decay), jnp.zeros_like(local_state))
    prefix = entering((block_decay, local_state), "ctx", combine_modes, neutral)
    incoming = prefix[1]
    from_start = powers * jnp.exp(-decay_rates)[None]
    carried = jnp.einsum(
        "tgn,gcn->tgc", from_start, incoming * mode_weight[:, None, :], precision=highest
    )
    mixed_conv = (medium_part + within + carried).reshape(row_count, channels)
    hidden = residual.astype(jnp.float32) + outer_feat * mixed_conv
    square_sum = lax.psum(jnp.sum(hidden * hidden, axis=1), "tp")
    normed = (
        hidden * norm_gain.astype(jnp.float32)[None, :] / jnp.sqrt(square_sum / D + 1e-05)[:, None]
    ).astype(jnp.bfloat16)
    return normed


def fused_kernel(
    n,
    tpn,
    outer_hbm,
    inner_hbm,
    value_hbm,
    taps_hbm,
    medium_hbm,
    decay_hbm,
    residues_hbm,
    residual_hbm,
    gain_hbm,
    out_ref,
    outer_ref,
    inner_ref,
    value_ref,
    taps_ref,
    medium_ref,
    decay_ref,
    residues_ref,
    residual_ref,
    gain_ref,
    decay_rows,
    weight_rows,
    halo_out,
    halo_in,
    gate_out,
    gate_in,
    ext_a,
    ext_b,
    prod_out,
    prod_all,
    medium_rev,
    filt_rev,
    toep,
    mixed_out,
    mixed_in,
    hidden,
    sq_out,
    sq_in,
    load_sem,
    halo_send,
    halo_recv,
    prod_send,
    prod_recv,
    mixed_send,
    mixed_recv,
    sq_send,
    sq_recv,
):
    f32 = jnp.float32
    me = lax.axis_index("ctx")
    tp_me = lax.axis_index("tp")
    rows, channels = outer_ref.shape
    width = channels // n
    mode_count = decay_ref.shape[0]
    group_width = channels // decay_ref.shape[1]
    group_count = width // group_width
    tap_count = taps_ref.shape[1]
    block_count = n * rows // BLOCK
    per_block = BLOCK // rows
    tile_groups = 128 // group_width
    half = channels // 2

    loads = [
        pltpu.make_async_copy(source, target, load_sem.at[index])
        for index, (source, target) in enumerate(
            [
                (inner_hbm, inner_ref),
                (value_hbm, value_ref),
                (outer_hbm, outer_ref),
                (decay_hbm, decay_ref),
                (residues_hbm, residues_ref),
                (medium_hbm, medium_ref),
                (taps_hbm, taps_ref),
                (residual_hbm, residual_ref),
                (gain_hbm, gain_ref),
            ]
        )
    ]
    for load in loads:
        load.start()

    barrier = pltpu.get_barrier_semaphore()

    def greet(k, carry):
        pl.semaphore_signal(
            barrier, inc=1, device_id={"ctx": lax.rem(me + k, n)}, device_id_type=MESH
        )
        return carry

    lax.fori_loop(1, n, greet, 0)
    for k in range(1, tpn):
        pl.semaphore_signal(
            barrier, inc=1, device_id={"tp": lax.rem(tp_me + k, tpn)}, device_id_type=MESH
        )

    def last_rows(ref, start, size):
        return ref[rows - 16 : rows, pl.ds(start, size)].astype(f32)[8:16]

    for load in loads[:3]:
        load.wait()
    for start in range(0, channels, 512):
        halo_out[:, pl.ds(start, 512)] = jnp.concatenate(
            [last_rows(inner_ref, start, 512), last_rows(value_ref, start, 512)], 0
        ).astype(jnp.bfloat16)
    for start in range(0, half, 512):
        gate_out[:, pl.ds(start, 512)] = jnp.concatenate(
            [last_rows(outer_ref, start, 512), last_rows(outer_ref, half + start, 512)], 0
        ).astype(jnp.bfloat16)

    pl.semaphore_wait(barrier, n - 1 + tpn - 1)

    def halo_copy(src, dst, index):
        return pltpu.make_async_remote_copy(
            src_ref=src,
            dst_ref=dst,
            send_sem=halo_send.at[index],
            recv_sem=halo_recv.at[index],
            device_id={"ctx": lax.rem(me + 1, n)},
            device_id_type=MESH,
        )

    halo_copies = [halo_copy(halo_out, halo_in, 0), halo_copy(gate_out, gate_in, 1)]

    @pl.when(me < n - 1)
    def _():
        for copy in halo_copies:
            copy.start()

    @pl.when(me == 0)
    def _():
        halo_in[...] = jnp.zeros_like(halo_in)
        gate_in[...] = jnp.zeros_like(gate_in)

    for load in loads[3:6]:
        load.wait()

    tap_index = lax.broadcasted_iota(jnp.int32, (BLOCK, BLOCK), 0)
    lane_index = lax.broadcasted_iota(jnp.int32, (BLOCK, BLOCK), 1)
    for m in range(2):
        pick = jnp.where(tap_index == BLOCK * m - lane_index, 1.0, 0.0).astype(jnp.bfloat16)
        medium_rev[m] = lax.dot_general(
            medium_ref[...], pick, (((0,), (0,)), ((), ())), preferred_element_type=f32
        )
    own_groups = pl.ds(pl.multiple_of(me * group_count, group_count), group_count)
    decay_rows[...] = decay_ref[...].T
    weight_rows[...] = (residues_ref[...] * jnp.sqrt(2.0 * decay_ref[...] / mode_count)).T
    decay = decay_rows[own_groups, :]
    weight = weight_rows[own_groups, :]
    lanes = lax.broadcasted_iota(jnp.int32, (group_count, BLOCK), 1)
    for m in range(block_count + 1):
        lag = BLOCK * m - lanes
        lag_rows = jnp.maximum(lag, 0).astype(f32)
        total = jnp.zeros((group_count, BLOCK), f32)
        for mode in range(mode_count):
            total = total + weight[:, mode : mode + 1] * jnp.exp(
                -decay[:, mode : mode + 1] * lag_rows
            )
        total = jnp.where(lag >= 0, total, 0.0)
        if m < 2:
            total = total + medium_rev[m, own_groups, :]
        filt_rev[m] = total

    def build(g, carry):
        block_rows = pl.ds(pl.multiple_of(g * BLOCK, BLOCK), BLOCK)
        upper = lane_index >= tap_index
        earlier = None
        for m in range(block_count + 1):
            row = jnp.broadcast_to(filt_rev[m, pl.ds(g, 1), :], (BLOCK, BLOCK))
            rolled = pltpu.roll(row, 0, 1, stride=1, stride_axis=0)
            if m > 0:
                place = (block_count - m) * BLOCK
                toep[block_rows, place : place + BLOCK] = jnp.where(
                    upper, earlier, rolled
                ).astype(jnp.bfloat16)
            earlier = rolled
        return carry

    lax.fori_loop(0, group_count, build, 0)

    for load in loads[6:]:
        load.wait()

    def featurize(which, ref, rim, ext, start, size):
        ext[0:8, :] = rim
        ext[8 : 8 + rows, :] = ref[:, pl.ds(start, size)].astype(f32)
        taps = taps_ref[which, :, pl.ds(start, size)].astype(f32)
        summed = taps[0:1] * ext[8 : 8 + rows, :]
        for offset in range(1, tap_count):
            summed = summed + taps[offset : offset + 1] * ext[8 - offset : 8 - offset + rows, :]
        return summed

    def product_for(owner):
        start = pl.multiple_of(owner * width, width)
        rim = halo_in[:, pl.ds(start, width)].astype(f32)
        inner_feat = featurize(1, inner_ref, rim[0:8], ext_a, start, width)
        value_feat = featurize(2, value_ref, rim[8:16], ext_b, start, width)
        return (inner_feat * value_feat).astype(jnp.bfloat16)

    def own_rows(place):
        return pl.ds(pl.multiple_of(place * rows, rows), rows)

    def product_copy(k):
        return pltpu.make_async_remote_copy(
            src_ref=prod_out.at[k],
            dst_ref=prod_all.at[own_rows(me)],
            send_sem=prod_send.at[k],
            recv_sem=prod_recv.at[k],
            device_id={"ctx": lax.rem(me + k, n)},
            device_id_type=MESH,
        )

    @pl.when(me > 0)
    def _():
        for copy in halo_copies:
            copy.wait_recv()

    def send_product(k, carry):
        prod_out[k] = product_for(lax.rem(me + k, n))
        product_copy(k).start()
        return carry

    lax.fori_loop(1, n, send_product, 0)
    prod_all[own_rows(me), :] = product_for(me)

    def gate_chunk(chunk, carry):
        start = pl.multiple_of(chunk * width, width)
        low = chunk < n // 2
        rim_start = pl.multiple_of(lax.rem(chunk, n // 2) * width, width)
        rim = gate_in[:, pl.ds(rim_start, width)].astype(f32)
        rim = jnp.where(low, rim[0:8], rim[8:16])
        hidden[:, pl.ds(start, width)] = featurize(0, outer_ref, rim, ext_a, start, width)
        return carry

    lax.fori_loop(0, n, gate_chunk, 0)

    def mixed_copy(place):
        return pltpu.make_async_remote_copy(
            src_ref=mixed_out.at[place],
            dst_ref=mixed_in.at[me],
            send_sem=mixed_send.at[place],
            recv_sem=mixed_recv.at[lax.rem(place - me + n, n)],
            device_id={"ctx": place},
            device_id_type=MESH,
        )

    lane_group = lax.broadcasted_iota(jnp.int32, (BLOCK, 128), 1) // group_width
    for block in range(block_count):
        for place in range(block * per_block, (block + 1) * per_block):

            @pl.when(me != place)
            def _():
                pltpu.make_async_remote_copy(
                    src_ref=prod_out.at[0],
                    dst_ref=prod_all.at[place * rows : (place + 1) * rows],
                    send_sem=prod_send.at[0],
                    recv_sem=prod_recv.at[lax.rem(me - place + n, n)],
                    device_id={"ctx": place},
                    device_id_type=MESH,
                ).wait_recv()

        depth = (block + 1) * BLOCK
        first = (block_count - 1 - block) * BLOCK

        for tile in range(width // 128):
            source = prod_all[0:depth, tile * 128 : (tile + 1) * 128]
            mixed = jnp.zeros((BLOCK, 128), f32)
            for part in range(0, tile_groups, 4):
                base = (tile * tile_groups + part) * BLOCK
                sums = jnp.dot(
                    toep[base : base + 4 * BLOCK, first:],
                    source,
                    preferred_element_type=f32,
                )
                for g in range(4):
                    mixed = jnp.where(
                        lane_group == part + g, sums[g * BLOCK : (g + 1) * BLOCK], mixed
                    )
            mixed = mixed.astype(jnp.bfloat16)
            for which in range(per_block):
                mixed_out[block * per_block + which, :, tile * 128 : (tile + 1) * 128] = mixed[
                    which * rows : (which + 1) * rows
                ]

        for place in range(block * per_block, (block + 1) * per_block):

            @pl.when(me != place)
            def _():
                mixed_copy(place).start()

            @pl.when(me == place)
            def _():
                mixed_in[place] = mixed_out[place]

    def gather_hidden(k, square):
        source = lax.rem(me - k + n, n)

        @pl.when(k > 0)
        def _():
            pltpu.make_async_remote_copy(
                src_ref=mixed_out.at[0],
                dst_ref=mixed_in.at[source],
                send_sem=mixed_send.at[0],
                recv_sem=mixed_recv.at[k],
                device_id={"ctx": source},
                device_id_type=MESH,
            ).wait_recv()

        chunk = pl.ds(pl.multiple_of(source * width, width), width)
        value = residual_ref[:, chunk].astype(f32) + hidden[:, chunk] * mixed_in[source].astype(f32)
        hidden[:, chunk] = value
        for tile in range(width // 128):
            piece = value[:, tile * 128 : (tile + 1) * 128]
            square = square + piece * piece
        return square

    square = lax.fori_loop(0, n, gather_hidden, jnp.zeros((rows, 128), f32))
    sq_out[...] = square

    def square_copy(k):
        return pltpu.make_async_remote_copy(
            src_ref=sq_out,
            dst_ref=sq_in.at[k],
            send_sem=sq_send.at[k],
            recv_sem=sq_recv.at[k],
            device_id={"tp": lax.rem(tp_me + k, tpn)},
            device_id_type=MESH,
        )

    for k in range(1, tpn):
        square_copy(k).start()
    for k in range(1, tpn):
        square_copy(k).wait_recv()
        square = square + sq_in[k]
    square_sum = jnp.sum(square, axis=1, keepdims=True)
    scale = 1.0 / jnp.sqrt(square_sum / (channels * tpn) + 1e-05)

    def finish(chunk, carry):
        start = pl.multiple_of(chunk * width, width)
        gain = gain_ref[pl.ds(start, width)].astype(f32).reshape(1, width)
        place = pl.ds(start, width)
        out_ref[:, place] = (hidden[:, place] * gain * scale).astype(jnp.bfloat16)
        return carry

    lax.fori_loop(0, n, finish, 0)

    @pl.when(me < n - 1)
    def _():
        for copy in halo_copies:
            copy.wait_send()

    def drain(k, carry):
        product_copy(k).wait_send()
        return carry

    lax.fori_loop(1, n, drain, 0)

    def drain_mixed(place, carry):
        @pl.when(me != place)
        def _():
            mixed_copy(place).wait_send()

        return carry

    lax.fori_loop(0, n, drain_mixed, 0)
    for k in range(1, tpn):
        square_copy(k).wait_send()


def fused(n, tpn, *args):
    outer_input, inner_input, value_input, taps, medium, decay, residues, residual, gain = args
    rows, channels = outer_input.shape
    width = channels // n
    all_groups, mode_count = decay.shape
    group_count = all_groups // n
    seq = n * rows
    blocks = seq // BLOCK
    bf16, f32 = jnp.bfloat16, jnp.float32
    dma = pltpu.SemaphoreType.DMA
    return pl.pallas_call(
        functools.partial(fused_kernel, n, tpn),
        out_shape=jax.ShapeDtypeStruct((rows, channels), bf16),
        in_specs=[pl.BlockSpec(memory_space=pltpu.HBM)] * 9,
        out_specs=pl.BlockSpec(memory_space=pltpu.VMEM),
        scratch_shapes=[
            pltpu.VMEM((rows, channels), bf16),
            pltpu.VMEM((rows, channels), bf16),
            pltpu.VMEM((rows, channels), bf16),
            pltpu.VMEM(taps.shape, bf16),
            pltpu.VMEM(medium.shape, bf16),
            pltpu.VMEM((mode_count, all_groups), f32),
            pltpu.VMEM((mode_count, all_groups), f32),
            pltpu.VMEM((rows, channels), bf16),
            pltpu.VMEM(gain.shape, bf16),
            pltpu.VMEM((all_groups, mode_count), f32),
            pltpu.VMEM((all_groups, mode_count), f32),
            pltpu.VMEM((16, channels), bf16),
            pltpu.VMEM((16, channels), bf16),
            pltpu.VMEM((16, channels // 2), bf16),
            pltpu.VMEM((16, channels // 2), bf16),
            pltpu.VMEM((rows + 8, width), f32),
            pltpu.VMEM((rows + 8, width), f32),
            pltpu.VMEM((n, rows, width), bf16),
            pltpu.VMEM((seq, width), bf16),
            pltpu.VMEM((2, decay.shape[0], BLOCK), f32),
            pltpu.VMEM((blocks + 1, group_count, BLOCK), f32),
            pltpu.VMEM((group_count * BLOCK, blocks * BLOCK), bf16),
            pltpu.VMEM((n, rows, width), bf16),
            pltpu.VMEM((n, rows, width), bf16),
            pltpu.VMEM((rows, channels), f32),
            pltpu.VMEM((rows, 128), f32),
            pltpu.VMEM((tpn, rows, 128), f32),
            dma((9,)),
            dma((2,)),
            dma((2,)),
            dma((n,)),
            dma((n,)),
            dma((n,)),
            dma((n,)),
            dma((tpn,)),
            dma((tpn,)),
        ],
        compiler_params=pltpu.CompilerParams(
            collective_id=0, has_side_effects=True, vmem_limit_bytes=63 * 1024 * 1024
        ),
    )(outer_input, inner_input, value_input, taps, medium, decay.T, residues.T, residual, gain)


def on_device(*args):
    n, tpn = lax.axis_size("ctx"), lax.axis_size("tp")
    rows, channels = args[0].shape
    medium_rows = args[4].shape[0]
    groups = args[5].shape[0]
    fits = (
        channels % (n * 128) == 0
        and BLOCK % rows == 0
        and rows % 16 == 0
        and groups % (8 * n) == 0
        and medium_rows == BLOCK
    )
    if fits:
        return fused(n, tpn, *args)
    return plain(*args)


def solution(mesh):
    return jax.shard_map(
        on_device,
        mesh=mesh,
        in_specs=(
            P("ctx", "tp"),
            P("ctx", "tp"),
            P("ctx", "tp"),
            P(None, None, "tp"),
            P(None, "tp"),
            P("tp", None),
            P("tp", None),
            P("ctx", "tp"),
            P("tp"),
        ),
        out_specs=P("ctx", "tp"),
        check_vma=False,
    )
```

```python
import functools
import jax
import jax.numpy as jnp
from jax import lax
from jax.experimental import pallas as pl
from jax.experimental.pallas import tpu as pltpu
from jax.sharding import PartitionSpec as P

MESH = pl.DeviceIdType.MESH
BLOCK = 128

D = 8192


def passed_along(array, axis, by):
    size = lax.axis_size(axis)
    pairs = [(i, i + by) for i in range(size) if 0 <= i + by < size]
    return lax.ppermute(array, axis, pairs)


def entering(part, axis, combine, identity):
    place = lax.axis_index(axis)
    gathered = jax.tree.map(lambda a: lax.all_gather(a, axis), part)
    state = jax.tree.map(lambda a, e: jnp.zeros_like(a) + jnp.asarray(e, a.dtype), part, identity)

    def one(lap, state):
        return combine(
            state, jax.tree.map(lambda a: lax.dynamic_index_in_dim(a, lap, 0, False), gathered)
        )

    return lax.fori_loop(0, place, one, state)


def banded(reversed_taps, row_count, width):
    group_count, tap_count = reversed_taps.shape
    period = width + 1
    padded = jnp.pad(reversed_taps, ((0, 0), (0, period - tap_count)))
    tiled = jnp.tile(padded, (1, row_count))
    return tiled[:, : row_count * width].reshape(group_count, row_count, width)


def featurize(extended, tap_table, row_count):
    rim_rows = tap_table.shape[0] - 1
    summed = jnp.zeros((row_count, extended.shape[1]), jnp.float32)
    for offset in range(tap_table.shape[0]):
        window = extended[rim_rows - offset : rim_rows - offset + row_count].astype(jnp.float32)
        summed = summed + tap_table[offset].astype(jnp.float32)[None, :] * window
    return summed


def product_rim(product, rim_depth):
    row_count = product.shape[0]
    pieces = []
    for distance in range(1, (rim_depth - 1) // row_count + 2):
        needed = min(row_count, rim_depth - (distance - 1) * row_count)
        arrived = passed_along(product[row_count - needed :], "ctx", distance)
        pieces = [arrived] + pieces
    return jnp.concatenate(pieces, 0)


def combine_modes(earlier, later):
    return (earlier[0] * later[0], earlier[1] * later[0] + later[1])


def plain(
    outer_input,
    inner_input,
    value_input,
    feature_taps,
    medium_taps,
    decay_rates,
    residues,
    residual,
    norm_gain,
):
    row_count, channels = outer_input.shape
    group_count, mode_count = decay_rates.shape
    group_width = channels // group_count
    feat_rim = feature_taps.shape[1] - 1
    medium_rim = medium_taps.shape[0] - 1
    highest = lax.Precision.HIGHEST
    rim_outer, rim_inner, rim_value = passed_along(
        (
            outer_input[row_count - feat_rim :],
            inner_input[row_count - feat_rim :],
            value_input[row_count - feat_rim :],
        ),
        "ctx",
        1,
    )
    inner_feat = featurize(jnp.concatenate([rim_inner, inner_input], 0), feature_taps[1], row_count)
    value_feat = featurize(jnp.concatenate([rim_value, value_input], 0), feature_taps[2], row_count)
    product = (inner_feat * value_feat).astype(jnp.bfloat16)
    extended = jnp.concatenate([product_rim(product, medium_rim), product], 0)
    outer_feat = featurize(jnp.concatenate([rim_outer, outer_input], 0), feature_taps[0], row_count)
    band_medium = banded(medium_taps[::-1].T, row_count, row_count + medium_rim)
    extended_groups = extended.reshape(row_count + medium_rim, group_count, group_width)
    medium_part = jnp.einsum(
        "gts,sgc->tgc", band_medium, extended_groups, preferred_element_type=jnp.float32
    )
    lag_rows = jnp.arange(row_count, dtype=jnp.float32)[:, None, None]
    mode_weight = residues * jnp.sqrt(2.0 * decay_rates / mode_count)
    powers = jnp.exp(-decay_rates[None] * lag_rows)
    long_taps = jnp.sum(powers * mode_weight[None], axis=2)
    band_long = banded(long_taps[::-1].T, row_count, 2 * row_count - 1)[:, :, row_count - 1 :]
    product_wide = product.reshape(row_count, group_count, group_width).astype(jnp.float32)
    within = jnp.einsum("gts,sgc->tgc", band_long, product_wide, precision=highest)
    to_end = jnp.exp(-decay_rates[None] * (row_count - 1.0 - lag_rows))
    local_state = jnp.einsum("tgc,tgn->gcn", product_wide, to_end, precision=highest)
    block_decay = jnp.exp(-decay_rates * row_count)[:, None, :]
    neutral = (jnp.ones_like(block_decay), jnp.zeros_like(local_state))
    prefix = entering((block_decay, local_state), "ctx", combine_modes, neutral)
    incoming = prefix[1]
    from_start = powers * jnp.exp(-decay_rates)[None]
    carried = jnp.einsum(
        "tgn,gcn->tgc", from_start, incoming * mode_weight[:, None, :], precision=highest
    )
    mixed_conv = (medium_part + within + carried).reshape(row_count, channels)
    hidden = residual.astype(jnp.float32) + outer_feat * mixed_conv
    square_sum = lax.psum(jnp.sum(hidden * hidden, axis=1), "tp")
    normed = (
        hidden * norm_gain.astype(jnp.float32)[None, :] / jnp.sqrt(square_sum / D + 1e-05)[:, None]
    ).astype(jnp.bfloat16)
    return normed


def fused_kernel(
    part,
    n,
    tpn,
    outer_hbm,
    inner_hbm,
    value_hbm,
    taps_hbm,
    medium_hbm,
    decay_hbm,
    residues_hbm,
    residual_hbm,
    gain_hbm,
    out_ref,
    outer_ref,
    inner_ref,
    value_ref,
    taps_ref,
    medium_ref,
    decay_ref,
    residues_ref,
    residual_ref,
    gain_ref,
    decay_rows,
    weight_rows,
    halo_out,
    halo_in,
    gate_out,
    gate_in,
    ext_a,
    ext_b,
    prod_out,
    prod_all,
    medium_rev,
    filt_rev,
    toep,
    decay_wide,
    weight_wide,
    carry_taps,
    carry_rows,
    state_taps,
    state_out,
    state_in,
    rim_in,
    mixed_sum,
    mixed_out,
    mixed_in,
    hidden,
    sq_out,
    sq_in,
    load_sem,
    halo_send,
    halo_recv,
    prod_send,
    prod_recv,
    mixed_send,
    mixed_recv,
    link_send,
    link_recv,
    sq_send,
    sq_recv,
):
    f32, bf16 = jnp.float32, jnp.bfloat16
    me = lax.axis_index("ctx")
    tp_me = lax.axis_index("tp")
    parts = n // part
    mine = me // part
    spot = lax.rem(me, part)
    rows, channels = outer_ref.shape
    width = channels // part
    mode_count, all_groups = decay_ref.shape
    group_width = channels // all_groups
    group_count = width // group_width
    tap_count = taps_ref.shape[1]
    tokens = part * rows
    block_count = tokens // BLOCK
    pair_count = block_count // 2
    tile_groups = 128 // group_width
    tile_count = width // 128
    half = channels // 2
    step = min(width, 256)

    loads = [
        pltpu.make_async_copy(source, target, load_sem.at[index])
        for index, (source, target) in enumerate(
            [
                (inner_hbm, inner_ref),
                (value_hbm, value_ref),
                (outer_hbm, outer_ref),
                (taps_hbm, taps_ref),
                (decay_hbm, decay_ref),
                (residues_hbm, residues_ref),
                (medium_hbm, medium_ref),
                (residual_hbm, residual_ref),
                (gain_hbm, gain_ref),
            ]
        )
    ]
    for load in loads:
        load.start()

    def peer(k):
        return {"ctx": mine * part + lax.rem(spot + k, part)}

    barrier = pltpu.get_barrier_semaphore()

    def signal(device):
        pl.semaphore_signal(barrier, inc=1, device_id=device, device_id_type=MESH)

    for k in range(1, part):
        signal(peer(k))
    for k in range(1, tpn):
        signal({"tp": lax.rem(tp_me + k, tpn)})
    if parts > 1:

        @pl.when(mine > 0)
        def _():
            signal({"ctx": lax.rem(me - part + n, n)})

            @pl.when(spot == 0)
            def _():
                signal({"ctx": lax.rem(me - 1 + n, n)})

    def last_rows(ref, start, size):
        return ref[rows - 16 : rows, pl.ds(start, size)].astype(f32)[8:16]

    for load in loads[:3]:
        load.wait()
    for start in range(0, channels, 512):
        halo_out[:, pl.ds(start, 512)] = jnp.concatenate(
            [last_rows(inner_ref, start, 512), last_rows(value_ref, start, 512)], 0
        ).astype(bf16)
    for start in range(0, half, 512):
        gate_out[:, pl.ds(start, 512)] = jnp.concatenate(
            [last_rows(outer_ref, start, 512), last_rows(outer_ref, half + start, 512)], 0
        ).astype(bf16)

    awaited = part - 1 + tpn - 1
    if parts > 1:
        awaited = awaited + (1 - mine // (parts - 1)) * (1 + (spot + 1) // part)
    pl.semaphore_wait(barrier, awaited)

    def halo_copy(src, dst, index):
        return pltpu.make_async_remote_copy(
            src_ref=src,
            dst_ref=dst,
            send_sem=halo_send.at[index],
            recv_sem=halo_recv.at[index],
            device_id={"ctx": lax.rem(me + 1, n)},
            device_id_type=MESH,
        )

    halo_copies = [halo_copy(halo_out, halo_in, 0), halo_copy(gate_out, gate_in, 1)]

    @pl.when(me < n - 1)
    def _():
        halo_copies[0].start()
        halo_copies[1].start()

    @pl.when(me == 0)
    def _():
        halo_in[...] = jnp.zeros_like(halo_in)
        gate_in[...] = jnp.zeros_like(gate_in)

    loads[3].wait()

    def windows(which, ext, start, size, first, count):
        taps = taps_ref[which, :, pl.ds(start, size)].astype(f32)
        summed = taps[0:1] * ext[first : first + count, :]
        for offset in range(1, tap_count):
            summed = summed + taps[offset : offset + 1] * ext[
                first - offset : first - offset + count, :
            ]
        return summed

    per_spot = width // step

    def lower_product(chunk, carry):
        start = pl.multiple_of(chunk * step, step)
        inside = pl.ds(pl.multiple_of(lax.rem(chunk, per_spot) * step, step), step)
        ext_a[8 : 8 + rows, :] = inner_ref[:, pl.ds(start, step)].astype(f32)
        ext_b[8 : 8 + rows, :] = value_ref[:, pl.ds(start, step)].astype(f32)
        inner_feat = windows(1, ext_a, start, step, 24, rows - 16)
        value_feat = windows(2, ext_b, start, step, 24, rows - 16)
        prod_out[chunk // per_spot, 16:rows, inside] = (inner_feat * value_feat).astype(bf16)
        return carry

    lax.fori_loop(0, channels // step, lower_product, 0)

    @pl.when(me > 0)
    def _():
        halo_copies[0].wait_recv()

    def upper_product(owner):
        for piece in range(per_spot):
            start = pl.multiple_of(owner * width + piece * step, step)
            rim = halo_in[:, pl.ds(start, step)].astype(f32)
            ext_a[0:8, :] = rim[0:8]
            ext_b[0:8, :] = rim[8:16]
            ext_a[8:24, :] = inner_ref[0:16, pl.ds(start, step)].astype(f32)
            ext_b[8:24, :] = value_ref[0:16, pl.ds(start, step)].astype(f32)
            inner_feat = windows(1, ext_a, start, step, 8, 16)
            value_feat = windows(2, ext_b, start, step, 8, 16)
            prod_out[owner, 0:16, piece * step : (piece + 1) * step] = (
                inner_feat * value_feat
            ).astype(bf16)

    def own_rows(place):
        return pl.ds(pl.multiple_of(BLOCK + place * rows, rows), rows)

    def product_copy(k):
        return pltpu.make_async_remote_copy(
            src_ref=prod_out.at[lax.rem(spot + k, part)],
            dst_ref=prod_all.at[own_rows(spot)],
            send_sem=prod_send.at[k],
            recv_sem=prod_recv.at[k],
            device_id=peer(k),
            device_id_type=MESH,
        )

    def send_product(k, carry):
        upper_product(lax.rem(spot + k, part))
        product_copy(k).start()
        return carry

    lax.fori_loop(1, part, send_product, 0)
    upper_product(spot)
    prod_all[own_rows(spot), :] = prod_out[spot]
    prod_all[0:BLOCK, :] = jnp.zeros((BLOCK, width), bf16)

    for load in loads[4:7]:
        load.wait()

    tap_index = lax.broadcasted_iota(jnp.int32, (BLOCK, BLOCK), 0)
    lane_index = lax.broadcasted_iota(jnp.int32, (BLOCK, BLOCK), 1)
    for m in range(2):
        pick = jnp.where(tap_index == BLOCK * m - lane_index, 1.0, 0.0).astype(bf16)
        medium_rev[m] = lax.dot_general(
            medium_ref[...], pick, (((0,), (0,)), ((), ())), preferred_element_type=f32
        )
    own_groups = pl.ds(pl.multiple_of(spot * group_count, group_count), group_count)
    decay_rows[...] = decay_ref[...].T
    weight_rows[...] = (residues_ref[...] * jnp.sqrt(2.0 * decay_ref[...] / mode_count)).T
    decay = decay_rows[own_groups, :]
    weight = weight_rows[own_groups, :]
    lanes = lax.broadcasted_iota(jnp.int32, (group_count, BLOCK), 1)
    for m in range(block_count + 1):
        lag = BLOCK * m - lanes
        lag_rows = jnp.maximum(lag, 0).astype(f32)
        total = jnp.zeros((group_count, BLOCK), f32)
        for mode in range(mode_count):
            total = total + weight[:, mode : mode + 1] * jnp.exp(
                -decay[:, mode : mode + 1] * lag_rows
            )
        total = jnp.where(lag >= 0, total, 0.0)
        if m < 2:
            total = total + medium_rev[m, own_groups, :]
        filt_rev[m] = total

    blank = jnp.zeros((group_count, 128 - 3 * mode_count), f32)
    decay_wide[...] = jnp.concatenate([decay, decay, decay, blank], 1)
    weight_wide[...] = jnp.concatenate([weight, weight, weight, blank], 1)

    mode_row = lax.broadcasted_iota(jnp.int32, (mode_count, 128), 0)
    mode_lane = lax.broadcasted_iota(jnp.int32, (mode_count, 128), 1)

    def decay_column(g):
        row = jnp.broadcast_to(decay_wide[pl.ds(g, 1), :], (mode_count, 128))
        return jnp.sum(jnp.where(mode_row == mode_lane, row, 0.0), axis=1, keepdims=True)

    def channel_decay(tile):
        spread = jnp.zeros((mode_count, 128), f32)
        for g in range(tile_groups):
            spread = jnp.where(
                mode_lane // group_width == g, decay_column(tile * tile_groups + g), spread
            )
        return spread

    if parts > 1:

        @pl.when(mine < parts - 1)
        def _():
            left = (
                tokens - 1 - lax.broadcasted_iota(jnp.int32, (mode_count, tokens), 1)
            ).astype(f32)

            def decays(g, carry):
                place = pl.ds(pl.multiple_of(g * mode_count, mode_count), mode_count)
                value = jnp.exp(-decay_column(g) * left)
                high = value.astype(bf16)
                state_taps[0, place, :] = high
                state_taps[1, place, :] = (value - high.astype(f32)).astype(bf16)
                return carry

            lax.fori_loop(0, group_count, decays, 0)

    upper = lane_index >= tap_index

    def build(g, carry):
        block_rows = pl.ds(pl.multiple_of(g * BLOCK, BLOCK), BLOCK)
        earlier = None
        for m in range(block_count + 1):
            row = jnp.broadcast_to(filt_rev[m, pl.ds(g, 1), :], (BLOCK, BLOCK))
            rolled = pltpu.roll(row, 0, 1, stride=1, stride_axis=0)
            if m > 0:
                place = (block_count - m) * BLOCK
                toep[block_rows, place : place + BLOCK] = jnp.where(
                    upper, earlier, rolled
                ).astype(bf16)
            earlier = rolled
        return carry

    lax.fori_loop(0, group_count, build, 0)

    if parts > 1:

        @pl.when(mine > 0)
        def _():
            carry_rows[...] = jnp.zeros_like(carry_rows)
            ahead = (tap_index + 1).astype(f32)

            def build_carry(g, carry):
                block_rows = pl.ds(pl.multiple_of(g * BLOCK, BLOCK), BLOCK)
                value = weight_wide[pl.ds(g, 1), :] * jnp.exp(-decay_wide[pl.ds(g, 1), :] * ahead)
                high = value.astype(bf16).astype(f32)
                carry_taps[block_rows, 0:BLOCK] = jnp.where(
                    lane_index < 2 * mode_count, high, value - high
                ).astype(bf16)
                row = medium_rev[1, pl.ds(spot * group_count + g, 1), :]
                rolled = pltpu.roll(
                    jnp.broadcast_to(row, (BLOCK, BLOCK)), 0, 1, stride=1, stride_axis=0
                )
                carry_taps[block_rows, BLOCK : 2 * BLOCK] = jnp.where(upper, rolled, 0.0).astype(
                    bf16
                )
                return carry

            lax.fori_loop(0, group_count, build_carry, 0)

    @pl.when(me > 0)
    def _():
        halo_copies[1].wait_recv()

    def gate_chunk(chunk, carry):
        start = pl.multiple_of(chunk * step, step)
        low = start < half
        rim_start = pl.multiple_of(lax.rem(start, half), step)
        rim = gate_in[:, pl.ds(rim_start, step)].astype(f32)
        ext_a[0:8, :] = jnp.where(low, rim[0:8], rim[8:16])
        ext_a[8 : 8 + rows, :] = outer_ref[:, pl.ds(start, step)].astype(f32)
        hidden[:, pl.ds(start, step)] = windows(0, ext_a, start, step, 8, rows)
        return carry

    lax.fori_loop(0, channels // step, gate_chunk, 0)

    def wait_product(place):
        @pl.when(spot != place)
        def _():
            pltpu.make_async_remote_copy(
                src_ref=prod_out.at[0],
                dst_ref=prod_all.at[BLOCK + place * rows : BLOCK + (place + 1) * rows],
                send_sem=prod_send.at[0],
                recv_sem=prod_recv.at[lax.rem(spot - place + part, part)],
                device_id=peer(1),
                device_id_type=MESH,
            ).wait_recv()

    def link_copy(src, dst, index):
        return pltpu.make_async_remote_copy(
            src_ref=src,
            dst_ref=dst,
            send_sem=link_send.at[index],
            recv_sem=link_recv.at[index],
            device_id={"ctx": lax.rem(me + part, n)},
            device_id_type=MESH,
        )

    rim_copy = link_copy(prod_all.at[tokens : tokens + BLOCK], rim_in, 0)
    state_copy = link_copy(state_out, state_in, 1)
    last_spots = range(part - BLOCK // rows, part)
    for place in last_spots:
        wait_product(place)
    if parts > 1:

        @pl.when(mine < parts - 1)
        def _():
            rim_copy.start()

    for place in range(part - BLOCK // rows):
        wait_product(place)

    if parts > 1:

        @pl.when(mine < parts - 1)
        def _():
            tile_rows = tile_groups * mode_count
            if parts > 2:

                @pl.when(mine > 0)
                def _():
                    state_copy.wait_recv()

            for tile in range(tile_count):
                place = slice(tile * 128, (tile + 1) * 128)
                source = prod_all[BLOCK : BLOCK + tokens, place]
                taps_rows = slice(tile * tile_rows, (tile + 1) * tile_rows)
                sums = jnp.dot(
                    state_taps[0, taps_rows, :], source, preferred_element_type=f32
                ) + jnp.dot(state_taps[1, taps_rows, :], source, preferred_element_type=f32)
                state = jnp.zeros((mode_count, 128), f32)
                for g in range(tile_groups):
                    state = jnp.where(
                        mode_lane // group_width == g,
                        sums[g * mode_count : (g + 1) * mode_count],
                        state,
                    )
                state_out[:, place] = state
            if parts > 2:

                @pl.when(mine > 0)
                def _():
                    for tile in range(tile_count):
                        place = slice(tile * 128, (tile + 1) * 128)
                        state_out[:, place] = state_out[:, place] + state_in[:, place] * jnp.exp(
                            -channel_decay(tile) * tokens
                        )

            state_copy.start()

    lane_group = lax.broadcasted_iota(jnp.int32, (BLOCK, 128), 1) // group_width

    def grouped(taps, columns, source, base):
        sums = [jnp.zeros((BLOCK, 128), f32)] * 2
        for first in range(0, tile_groups, 4):
            start = pl.multiple_of(base + first * BLOCK, BLOCK)
            result = jnp.dot(
                taps[pl.ds(start, 4 * BLOCK), columns], source, preferred_element_type=f32
            )
            for g in range(4):
                for side in range(2):
                    sums[side] = jnp.where(
                        lane_group == first + g,
                        result[g * BLOCK : (g + 1) * BLOCK, side * 128 : (side + 1) * 128],
                        sums[side],
                    )
        return sums

    def own_part(tile, carry):
        place = pl.ds(pl.multiple_of(tile * 128, 128), 128)
        base = tile * tile_groups * BLOCK
        for pair in range(pair_count):
            depth = (pair + 1) * 2 * BLOCK
            columns = slice(block_count * BLOCK - depth, block_count * BLOCK)
            source = jnp.concatenate(
                [prod_all[0:depth, place], prod_all[BLOCK : BLOCK + depth, place]], 1
            )
            sums = grouped(toep, columns, source, base)
            for side in range(2):
                at = (pair * 2 + side) * BLOCK
                mixed_sum[at : at + BLOCK, place] = sums[side]
        return carry

    lax.fori_loop(0, tile_count, own_part, 0)

    def mixed_copy(place):
        return pltpu.make_async_remote_copy(
            src_ref=mixed_out.at[place],
            dst_ref=mixed_in.at[spot],
            send_sem=mixed_send.at[place],
            recv_sem=mixed_recv.at[lax.rem(place - spot + part, part)],
            device_id={"ctx": mine * part + place},
            device_id_type=MESH,
        )

    if parts > 1:

        @pl.when(mine > 0)
        def _():
            rim_copy.wait_recv()
            if parts > 2:

                @pl.when(mine == parts - 1)
                def _():
                    state_copy.wait_recv()

            else:
                state_copy.wait_recv()

            for tile in range(tile_count):
                place = slice(tile * 128, (tile + 1) * 128)
                fade = channel_decay(tile)
                carry_rows[0, BLOCK : 2 * BLOCK, tile * 256 : tile * 256 + 128] = rim_in[:, place]
                for block in range(block_count):
                    state = state_in[:, place] * jnp.exp(-fade * (block * BLOCK))
                    high = state.astype(bf16)
                    low = (state - high.astype(f32)).astype(bf16)
                    at = tile * 256 + block % 2 * 128
                    carry_rows[block // 2, 0 : 3 * mode_count, at : at + 128] = jnp.concatenate(
                        [high, low, high], 0
                    )

    pair_spots = 2 * BLOCK // rows
    for pair in range(pair_count):
        if parts > 1:

            @pl.when(mine > 0)
            def _():
                depth = 2 * BLOCK if pair == 0 else BLOCK

                def carried(tile, carry):
                    place = pl.ds(pl.multiple_of(tile * 128, 128), 128)
                    source = carry_rows[
                        pair, 0:depth, pl.ds(pl.multiple_of(tile * 256, 256), 256)
                    ]
                    sums = grouped(
                        carry_taps, slice(0, depth), source, tile * tile_groups * BLOCK
                    )
                    for side in range(2):
                        at = (pair * 2 + side) * BLOCK
                        mixed_sum[at : at + BLOCK, place] += sums[side]
                    return carry

                lax.fori_loop(0, tile_count, carried, 0)

        for place in range(pair * pair_spots, (pair + 1) * pair_spots):
            mixed_out[place] = mixed_sum[place * rows : (place + 1) * rows, :].astype(bf16)

            @pl.when(spot != place)
            def _():
                mixed_copy(place).start()

            @pl.when(spot == place)
            def _():
                mixed_in[place] = mixed_out[place]

    loads[7].wait()
    loads[8].wait()

    def gather_hidden(k, square):
        source = lax.rem(spot - k + part, part)

        @pl.when(k > 0)
        def _():
            pltpu.make_async_remote_copy(
                src_ref=mixed_out.at[0],
                dst_ref=mixed_in.at[source],
                send_sem=mixed_send.at[0],
                recv_sem=mixed_recv.at[k],
                device_id=peer(1),
                device_id_type=MESH,
            ).wait_recv()

        for piece in range(per_spot):
            inside = slice(piece * step, (piece + 1) * step)
            chunk = pl.ds(pl.multiple_of(source * width + piece * step, step), step)
            value = residual_ref[:, chunk].astype(f32) + hidden[:, chunk] * mixed_in[
                source, :, inside
            ].astype(f32)
            hidden[:, chunk] = value
            for tile in range(step // 128):
                cut = value[:, tile * 128 : (tile + 1) * 128]
                square = square + cut * cut
        return square

    square = lax.fori_loop(0, part, gather_hidden, jnp.zeros((rows, 128), f32))
    sq_out[...] = square

    def square_copy(k):
        return pltpu.make_async_remote_copy(
            src_ref=sq_out,
            dst_ref=sq_in.at[k],
            send_sem=sq_send.at[k],
            recv_sem=sq_recv.at[k],
            device_id={"tp": lax.rem(tp_me + k, tpn)},
            device_id_type=MESH,
        )

    for k in range(1, tpn):
        square_copy(k).start()
    for k in range(1, tpn):
        square_copy(k).wait_recv()
        square = square + sq_in[k]
    square_sum = jnp.sum(square, axis=1, keepdims=True)
    scale = 1.0 / jnp.sqrt(square_sum / (channels * tpn) + 1e-05)

    def finish(chunk, carry):
        start = pl.multiple_of(chunk * 256, 256)
        gain = gain_ref[pl.ds(start, 256)].astype(f32).reshape(1, 256)
        place = pl.ds(start, 256)
        out_ref[:, place] = (hidden[:, place] * gain * scale).astype(bf16)
        return carry

    lax.fori_loop(0, channels // 256, finish, 0)

    @pl.when(me < n - 1)
    def _():
        for copy in halo_copies:
            copy.wait_send()

    if parts > 1:

        @pl.when(mine < parts - 1)
        def _():
            rim_copy.wait_send()
            state_copy.wait_send()

    for k in range(1, part):
        product_copy(k).wait_send()
    for place in range(part):

        @pl.when(spot != place)
        def _():
            mixed_copy(place).wait_send()

    for k in range(1, tpn):
        square_copy(k).wait_send()


def fused(part, n, tpn, *args):
    outer_input, inner_input, value_input, taps, medium, decay, residues, residual, gain = args
    rows, channels = outer_input.shape
    width = channels // part
    all_groups, mode_count = decay.shape
    group_count = all_groups // part
    tokens = part * rows
    blocks = tokens // BLOCK
    step = min(width, 256)
    bf16, f32 = jnp.bfloat16, jnp.float32
    dma = pltpu.SemaphoreType.DMA
    return pl.pallas_call(
        functools.partial(fused_kernel, part, n, tpn),
        out_shape=jax.ShapeDtypeStruct((rows, channels), bf16),
        in_specs=[pl.BlockSpec(memory_space=pltpu.HBM)] * 9,
        out_specs=pl.BlockSpec(memory_space=pltpu.VMEM),
        scratch_shapes=[
            pltpu.VMEM((rows, channels), bf16),
            pltpu.VMEM((rows, channels), bf16),
            pltpu.VMEM((rows, channels), bf16),
            pltpu.VMEM(taps.shape, bf16),
            pltpu.VMEM(medium.shape, bf16),
            pltpu.VMEM((mode_count, all_groups), f32),
            pltpu.VMEM((mode_count, all_groups), f32),
            pltpu.VMEM((rows, channels), bf16),
            pltpu.VMEM(gain.shape, bf16),
            pltpu.VMEM((all_groups, mode_count), f32),
            pltpu.VMEM((all_groups, mode_count), f32),
            pltpu.VMEM((16, channels), bf16),
            pltpu.VMEM((16, channels), bf16),
            pltpu.VMEM((16, channels // 2), bf16),
            pltpu.VMEM((16, channels // 2), bf16),
            pltpu.VMEM((rows + 8, step), f32),
            pltpu.VMEM((rows + 8, step), f32),
            pltpu.VMEM((part, rows, width), bf16),
            pltpu.VMEM((BLOCK + tokens, width), bf16),
            pltpu.VMEM((2, all_groups, BLOCK), f32),
            pltpu.VMEM((blocks + 1, group_count, BLOCK), f32),
            pltpu.VMEM((group_count * BLOCK, tokens), bf16),
            pltpu.VMEM((group_count, 128), f32),
            pltpu.VMEM((group_count, 128), f32),
            pltpu.VMEM((group_count * BLOCK, 2 * BLOCK), bf16),
            pltpu.VMEM((blocks // 2, 2 * BLOCK, 2 * width), bf16),
            pltpu.VMEM((2, group_count * mode_count, tokens), bf16),
            pltpu.VMEM((mode_count, width), f32),
            pltpu.VMEM((mode_count, width), f32),
            pltpu.VMEM((BLOCK, width), bf16),
            pltpu.VMEM((tokens, width), f32),
            pltpu.VMEM((part, rows, width), bf16),
            pltpu.VMEM((part, rows, width), bf16),
            pltpu.VMEM((rows, channels), f32),
            pltpu.VMEM((rows, 128), f32),
            pltpu.VMEM((tpn, rows, 128), f32),
            dma((9,)),
            dma((2,)),
            dma((2,)),
            dma((part,)),
            dma((part,)),
            dma((part,)),
            dma((part,)),
            dma((2,)),
            dma((2,)),
            dma((tpn,)),
            dma((tpn,)),
        ],
        compiler_params=pltpu.CompilerParams(
            collective_id=0, has_side_effects=True, vmem_limit_bytes=63 * 1024 * 1024
        ),
    )(outer_input, inner_input, value_input, taps, medium, decay.T, residues.T, residual, gain)


PART = 8


def on_device(*args):
    n, tpn = lax.axis_size("ctx"), lax.axis_size("tp")
    rows, channels = args[0].shape
    taps_rows, medium_rows = args[3].shape[1], args[4].shape[0]
    groups, modes = args[5].shape
    fits = (
        n % PART == 0
        and channels % (PART * 128) == 0
        and channels % 1024 == 0
        and BLOCK % rows == 0
        and rows % 32 == 0
        and (PART * rows) % (2 * BLOCK) == 0
        and groups % (8 * PART) == 0
        and 128 % (channels // groups) == 0
        and channels // groups <= 32
        and modes % 16 == 0
        and modes <= 32
        and taps_rows <= 9
        and medium_rows == BLOCK
    )
    if fits:
        return fused(PART, n, tpn, *args)
    return plain(*args)


def solution(mesh):
    return jax.shard_map(
        on_device,
        mesh=mesh,
        in_specs=(
            P("ctx", "tp"),
            P("ctx", "tp"),
            P("ctx", "tp"),
            P(None, None, "tp"),
            P(None, "tp"),
            P("tp", None),
            P("tp", None),
            P("ctx", "tp"),
            P("tp"),
        ),
        out_specs=P("ctx", "tp"),
        check_vma=False,
    )
```

```python
import functools
import jax
import jax.numpy as jnp
from jax import lax
from jax.experimental import pallas as pl
from jax.experimental.pallas import tpu as pltpu
from jax.sharding import PartitionSpec as P

MESH = pl.DeviceIdType.MESH
BLOCK = 128

D = 8192


def passed_along(array, axis, by):
    size = lax.axis_size(axis)
    pairs = [(i, i + by) for i in range(size) if 0 <= i + by < size]
    return lax.ppermute(array, axis, pairs)


def entering(part, axis, combine, identity):
    place = lax.axis_index(axis)
    gathered = jax.tree.map(lambda a: lax.all_gather(a, axis), part)
    state = jax.tree.map(lambda a, e: jnp.zeros_like(a) + jnp.asarray(e, a.dtype), part, identity)

    def one(lap, state):
        return combine(
            state, jax.tree.map(lambda a: lax.dynamic_index_in_dim(a, lap, 0, False), gathered)
        )

    return lax.fori_loop(0, place, one, state)


def banded(reversed_taps, row_count, width):
    group_count, tap_count = reversed_taps.shape
    period = width + 1
    padded = jnp.pad(reversed_taps, ((0, 0), (0, period - tap_count)))
    tiled = jnp.tile(padded, (1, row_count))
    return tiled[:, : row_count * width].reshape(group_count, row_count, width)


def featurize(extended, tap_table, row_count):
    rim_rows = tap_table.shape[0] - 1
    summed = jnp.zeros((row_count, extended.shape[1]), jnp.float32)
    for offset in range(tap_table.shape[0]):
        window = extended[rim_rows - offset : rim_rows - offset + row_count].astype(jnp.float32)
        summed = summed + tap_table[offset].astype(jnp.float32)[None, :] * window
    return summed


def product_rim(product, rim_depth):
    row_count = product.shape[0]
    pieces = []
    for distance in range(1, (rim_depth - 1) // row_count + 2):
        needed = min(row_count, rim_depth - (distance - 1) * row_count)
        arrived = passed_along(product[row_count - needed :], "ctx", distance)
        pieces = [arrived] + pieces
    return jnp.concatenate(pieces, 0)


def combine_modes(earlier, later):
    return (earlier[0] * later[0], earlier[1] * later[0] + later[1])


def plain(
    outer_input,
    inner_input,
    value_input,
    feature_taps,
    medium_taps,
    decay_rates,
    residues,
    residual,
    norm_gain,
):
    row_count, channels = outer_input.shape
    group_count, mode_count = decay_rates.shape
    group_width = channels // group_count
    feat_rim = feature_taps.shape[1] - 1
    medium_rim = medium_taps.shape[0] - 1
    highest = lax.Precision.HIGHEST
    rim_outer, rim_inner, rim_value = passed_along(
        (
            outer_input[row_count - feat_rim :],
            inner_input[row_count - feat_rim :],
            value_input[row_count - feat_rim :],
        ),
        "ctx",
        1,
    )
    inner_feat = featurize(jnp.concatenate([rim_inner, inner_input], 0), feature_taps[1], row_count)
    value_feat = featurize(jnp.concatenate([rim_value, value_input], 0), feature_taps[2], row_count)
    product = (inner_feat * value_feat).astype(jnp.bfloat16)
    extended = jnp.concatenate([product_rim(product, medium_rim), product], 0)
    outer_feat = featurize(jnp.concatenate([rim_outer, outer_input], 0), feature_taps[0], row_count)
    band_medium = banded(medium_taps[::-1].T, row_count, row_count + medium_rim)
    extended_groups = extended.reshape(row_count + medium_rim, group_count, group_width)
    medium_part = jnp.einsum(
        "gts,sgc->tgc", band_medium, extended_groups, preferred_element_type=jnp.float32
    )
    lag_rows = jnp.arange(row_count, dtype=jnp.float32)[:, None, None]
    mode_weight = residues * jnp.sqrt(2.0 * decay_rates / mode_count)
    powers = jnp.exp(-decay_rates[None] * lag_rows)
    long_taps = jnp.sum(powers * mode_weight[None], axis=2)
    band_long = banded(long_taps[::-1].T, row_count, 2 * row_count - 1)[:, :, row_count - 1 :]
    product_wide = product.reshape(row_count, group_count, group_width).astype(jnp.float32)
    within = jnp.einsum("gts,sgc->tgc", band_long, product_wide, precision=highest)
    to_end = jnp.exp(-decay_rates[None] * (row_count - 1.0 - lag_rows))
    local_state = jnp.einsum("tgc,tgn->gcn", product_wide, to_end, precision=highest)
    block_decay = jnp.exp(-decay_rates * row_count)[:, None, :]
    neutral = (jnp.ones_like(block_decay), jnp.zeros_like(local_state))
    prefix = entering((block_decay, local_state), "ctx", combine_modes, neutral)
    incoming = prefix[1]
    from_start = powers * jnp.exp(-decay_rates)[None]
    carried = jnp.einsum(
        "tgn,gcn->tgc", from_start, incoming * mode_weight[:, None, :], precision=highest
    )
    mixed_conv = (medium_part + within + carried).reshape(row_count, channels)
    hidden = residual.astype(jnp.float32) + outer_feat * mixed_conv
    square_sum = lax.psum(jnp.sum(hidden * hidden, axis=1), "tp")
    normed = (
        hidden * norm_gain.astype(jnp.float32)[None, :] / jnp.sqrt(square_sum / D + 1e-05)[:, None]
    ).astype(jnp.bfloat16)
    return normed


def fused_kernel(
    part,
    n,
    tpn,
    outer_hbm,
    inner_hbm,
    value_hbm,
    taps_hbm,
    medium_hbm,
    decay_hbm,
    residues_hbm,
    residual_hbm,
    gain_hbm,
    out_ref,
    outer_ref,
    inner_ref,
    value_ref,
    taps_ref,
    medium_ref,
    decay_ref,
    residues_ref,
    residual_ref,
    gain_ref,
    decay_rows,
    weight_rows,
    halo_out,
    halo_in,
    gate_out,
    gate_in,
    ext_a,
    ext_b,
    prod_out,
    prod_all,
    medium_rev,
    filt_rev,
    toep,
    decay_wide,
    weight_wide,
    carry_taps,
    carry_rows,
    state_taps,
    state_out,
    state_in,
    rim_in,
    mixed_sum,
    mixed_out,
    mixed_in,
    hidden,
    sq_out,
    sq_in,
    load_sem,
    halo_send,
    halo_recv,
    prod_send,
    prod_recv,
    mixed_send,
    mixed_recv,
    link_send,
    link_recv,
    sq_send,
    sq_recv,
):
    f32, bf16 = jnp.float32, jnp.bfloat16
    me = lax.axis_index("ctx")
    tp_me = lax.axis_index("tp")
    parts = n // part
    mine = me // part
    spot = lax.rem(me, part)
    rows, channels = outer_ref.shape
    width = channels // part
    mode_count, all_groups = decay_ref.shape
    group_width = channels // all_groups
    group_count = width // group_width
    tap_count = taps_ref.shape[1]
    tokens = part * rows
    block_count = tokens // BLOCK
    pair_count = block_count // 2
    tile_groups = 128 // group_width
    tile_count = width // 128
    half = channels // 2
    step = 128

    loads = [
        pltpu.make_async_copy(source, target, load_sem.at[index])
        for index, (source, target) in enumerate(
            [
                (inner_hbm, inner_ref),
                (value_hbm, value_ref),
                (outer_hbm, outer_ref),
                (taps_hbm, taps_ref),
                (decay_hbm, decay_ref),
                (residues_hbm, residues_ref),
                (medium_hbm, medium_ref),
                (residual_hbm, residual_ref),
                (gain_hbm, gain_ref),
            ]
        )
    ]
    for load in loads:
        load.start()

    def peer(k):
        return {"ctx": mine * part + lax.rem(spot + k, part)}

    barrier = pltpu.get_barrier_semaphore()

    def signal(device):
        pl.semaphore_signal(barrier, inc=1, device_id=device, device_id_type=MESH)

    for k in range(1, part):
        signal(peer(k))
    for k in range(1, tpn):
        signal({"tp": lax.rem(tp_me + k, tpn)})
    if parts > 1:

        @pl.when(mine > 0)
        def _():
            signal({"ctx": lax.rem(me - part + n, n)})

            @pl.when(spot == 0)
            def _():
                signal({"ctx": lax.rem(me - 1 + n, n)})

    def last_rows(ref, start, size):
        return ref[rows - 16 : rows, pl.ds(start, size)].astype(f32)[8:16]

    for load in loads[:3]:
        load.wait()
    for start in range(0, channels, 512):
        halo_out[:, pl.ds(start, 512)] = jnp.concatenate(
            [last_rows(inner_ref, start, 512), last_rows(value_ref, start, 512)], 0
        ).astype(bf16)
    for start in range(0, half, 512):
        gate_out[:, pl.ds(start, 512)] = jnp.concatenate(
            [last_rows(outer_ref, start, 512), last_rows(outer_ref, half + start, 512)], 0
        ).astype(bf16)

    awaited = part - 1 + tpn - 1
    if parts > 1:
        awaited = awaited + (1 - mine // (parts - 1)) * (1 + (spot + 1) // part)
    pl.semaphore_wait(barrier, awaited)

    def halo_copy(src, dst, index):
        return pltpu.make_async_remote_copy(
            src_ref=src,
            dst_ref=dst,
            send_sem=halo_send.at[index],
            recv_sem=halo_recv.at[index],
            device_id={"ctx": lax.rem(me + 1, n)},
            device_id_type=MESH,
        )

    halo_copies = [halo_copy(halo_out, halo_in, 0), halo_copy(gate_out, gate_in, 1)]

    @pl.when(me < n - 1)
    def _():
        halo_copies[0].start()
        halo_copies[1].start()

    @pl.when(me == 0)
    def _():
        halo_in[...] = jnp.zeros_like(halo_in)
        gate_in[...] = jnp.zeros_like(gate_in)

    loads[3].wait()

    def windows(which, ext, start, size, first, count):
        taps = taps_ref[which, :, pl.ds(start, size)].astype(f32)
        summed = taps[0:1] * ext[first : first + count, :]
        for offset in range(1, tap_count):
            summed = summed + taps[offset : offset + 1] * ext[
                first - offset : first - offset + count, :
            ]
        return summed

    per_spot = width // step

    def lower_product(chunk, carry):
        start = pl.multiple_of(chunk * step, step)
        inside = pl.ds(pl.multiple_of(lax.rem(chunk, per_spot) * step, step), step)
        ext_a[8 : 8 + rows, :] = inner_ref[:, pl.ds(start, step)].astype(f32)
        ext_b[8 : 8 + rows, :] = value_ref[:, pl.ds(start, step)].astype(f32)
        inner_feat = windows(1, ext_a, start, step, 24, rows - 16)
        value_feat = windows(2, ext_b, start, step, 24, rows - 16)
        prod_out[chunk // per_spot, 16:rows, inside] = (inner_feat * value_feat).astype(bf16)
        return carry

    lax.fori_loop(0, channels // step, lower_product, 0)

    @pl.when(me > 0)
    def _():
        halo_copies[0].wait_recv()

    def upper_product(owner):
        for piece in range(per_spot):
            start = pl.multiple_of(owner * width + piece * step, step)
            rim = halo_in[:, pl.ds(start, step)].astype(f32)
            ext_a[0:8, :] = rim[0:8]
            ext_b[0:8, :] = rim[8:16]
            ext_a[8:24, :] = inner_ref[0:16, pl.ds(start, step)].astype(f32)
            ext_b[8:24, :] = value_ref[0:16, pl.ds(start, step)].astype(f32)
            inner_feat = windows(1, ext_a, start, step, 8, 16)
            value_feat = windows(2, ext_b, start, step, 8, 16)
            prod_out[owner, 0:16, piece * step : (piece + 1) * step] = (
                inner_feat * value_feat
            ).astype(bf16)

    def own_rows(place):
        return pl.ds(pl.multiple_of(BLOCK + place * rows, rows), rows)

    def product_copy(k):
        return pltpu.make_async_remote_copy(
            src_ref=prod_out.at[lax.rem(spot + k, part)],
            dst_ref=prod_all.at[own_rows(spot)],
            send_sem=prod_send.at[k],
            recv_sem=prod_recv.at[k],
            device_id=peer(k),
            device_id_type=MESH,
        )

    def send_product(k, carry):
        upper_product(lax.rem(spot + k, part))
        product_copy(k).start()
        return carry

    lax.fori_loop(1, part, send_product, 0)
    upper_product(spot)
    prod_all[own_rows(spot), :] = prod_out[spot]
    prod_all[0:BLOCK, :] = jnp.zeros((BLOCK, width), bf16)

    for load in loads[4:7]:
        load.wait()

    tap_index = lax.broadcasted_iota(jnp.int32, (BLOCK, BLOCK), 0)
    lane_index = lax.broadcasted_iota(jnp.int32, (BLOCK, BLOCK), 1)
    for m in range(2):
        pick = jnp.where(tap_index == BLOCK * m - lane_index, 1.0, 0.0).astype(bf16)
        medium_rev[m] = lax.dot_general(
            medium_ref[...], pick, (((0,), (0,)), ((), ())), preferred_element_type=f32
        )
    own_groups = pl.ds(pl.multiple_of(spot * group_count, group_count), group_count)
    decay_rows[...] = decay_ref[...].T
    weight_rows[...] = (residues_ref[...] * jnp.sqrt(2.0 * decay_ref[...] / mode_count)).T
    decay = decay_rows[own_groups, :]
    weight = weight_rows[own_groups, :]
    lanes = lax.broadcasted_iota(jnp.int32, (group_count, BLOCK), 1)
    for m in range(block_count + 1):
        lag = BLOCK * m - lanes
        lag_rows = jnp.maximum(lag, 0).astype(f32)
        total = jnp.zeros((group_count, BLOCK), f32)
        for mode in range(mode_count):
            total = total + weight[:, mode : mode + 1] * jnp.exp(
                -decay[:, mode : mode + 1] * lag_rows
            )
        total = jnp.where(lag >= 0, total, 0.0)
        if m < 2:
            total = total + medium_rev[m, own_groups, :]
        filt_rev[m] = total

    blank = jnp.zeros((group_count, 128 - 3 * mode_count), f32)
    decay_wide[...] = jnp.concatenate([decay, decay, decay, blank], 1)
    weight_wide[...] = jnp.concatenate([weight, weight, weight, blank], 1)

    mode_row = lax.broadcasted_iota(jnp.int32, (mode_count, 128), 0)
    mode_lane = lax.broadcasted_iota(jnp.int32, (mode_count, 128), 1)

    def decay_column(g):
        row = jnp.broadcast_to(decay_wide[pl.ds(g, 1), :], (mode_count, 128))
        return jnp.sum(jnp.where(mode_row == mode_lane, row, 0.0), axis=1, keepdims=True)

    def channel_decay(tile):
        spread = jnp.zeros((mode_count, 128), f32)
        for g in range(tile_groups):
            spread = jnp.where(
                mode_lane // group_width == g, decay_column(tile * tile_groups + g), spread
            )
        return spread

    if parts > 1:

        @pl.when(mine < parts - 1)
        def _():
            left = (
                tokens - 1 - lax.broadcasted_iota(jnp.int32, (mode_count, tokens), 1)
            ).astype(f32)

            def decays(g, carry):
                place = pl.ds(pl.multiple_of(g * mode_count, mode_count), mode_count)
                value = jnp.exp(-decay_column(g) * left)
                high = value.astype(bf16)
                state_taps[0, place, :] = high
                state_taps[1, place, :] = (value - high.astype(f32)).astype(bf16)
                return carry

            lax.fori_loop(0, group_count, decays, 0)

    @pl.when(me > 0)
    def _():
        halo_copies[1].wait_recv()

    def gate_chunk(chunk, carry):
        start = pl.multiple_of(chunk * step, step)
        low = start < half
        rim_start = pl.multiple_of(lax.rem(start, half), step)
        rim = gate_in[:, pl.ds(rim_start, step)].astype(f32)
        ext_a[0:8, :] = jnp.where(low, rim[0:8], rim[8:16])
        ext_a[8 : 8 + rows, :] = outer_ref[:, pl.ds(start, step)].astype(f32)
        hidden[:, pl.ds(start, step)] = windows(0, ext_a, start, step, 8, rows)
        return carry

    lax.fori_loop(0, channels // step, gate_chunk, 0)

    def wait_product(place):
        @pl.when(spot != place)
        def _():
            pltpu.make_async_remote_copy(
                src_ref=prod_out.at[0],
                dst_ref=prod_all.at[BLOCK + place * rows : BLOCK + (place + 1) * rows],
                send_sem=prod_send.at[0],
                recv_sem=prod_recv.at[lax.rem(spot - place + part, part)],
                device_id=peer(1),
                device_id_type=MESH,
            ).wait_recv()

    def link_copy(src, dst, index):
        return pltpu.make_async_remote_copy(
            src_ref=src,
            dst_ref=dst,
            send_sem=link_send.at[index],
            recv_sem=link_recv.at[index],
            device_id={"ctx": lax.rem(me + part, n)},
            device_id_type=MESH,
        )

    rim_copy = link_copy(prod_all.at[tokens : tokens + BLOCK], rim_in, 0)
    state_copy = link_copy(state_out, state_in, 1)
    rim_spots = part - BLOCK // rows

    if parts > 1:

        @pl.when(mine < parts - 1)
        def _():
            for place in range(rim_spots, part):
                wait_product(place)
            rim_copy.start()
            for place in range(rim_spots):
                wait_product(place)
            tile_rows = tile_groups * mode_count
            for tile in range(tile_count):
                place = slice(tile * 128, (tile + 1) * 128)
                source = prod_all[BLOCK : BLOCK + tokens, place]
                taps_rows = slice(tile * tile_rows, (tile + 1) * tile_rows)
                sums = jnp.dot(
                    state_taps[0, taps_rows, :], source, preferred_element_type=f32
                ) + jnp.dot(state_taps[1, taps_rows, :], source, preferred_element_type=f32)
                state = jnp.zeros((mode_count, 128), f32)
                for g in range(tile_groups):
                    state = jnp.where(
                        mode_lane // group_width == g,
                        sums[g * mode_count : (g + 1) * mode_count],
                        state,
                    )
                state_out[:, place] = state
            if parts > 2:

                @pl.when(mine > 0)
                def _():
                    state_copy.wait_recv()
                    for tile in range(tile_count):
                        place = slice(tile * 128, (tile + 1) * 128)
                        state_out[:, place] = state_out[:, place] + state_in[:, place] * jnp.exp(
                            -channel_decay(tile) * tokens
                        )

            state_copy.start()

    upper = lane_index >= tap_index

    def build(g, carry):
        block_rows = pl.ds(pl.multiple_of(g * BLOCK, BLOCK), BLOCK)
        earlier = None
        for m in range(block_count + 1):
            row = jnp.broadcast_to(filt_rev[m, pl.ds(g, 1), :], (BLOCK, BLOCK))
            rolled = pltpu.roll(row, 0, 1, stride=1, stride_axis=0)
            if m > 0:
                place = (block_count - m) * BLOCK
                toep[block_rows, place : place + BLOCK] = jnp.where(
                    upper, earlier, rolled
                ).astype(bf16)
            earlier = rolled
        return carry

    lax.fori_loop(0, group_count, build, 0)

    if parts > 1:

        @pl.when(mine > 0)
        def _():
            carry_rows[...] = jnp.zeros_like(carry_rows)
            ahead = (tap_index + 1).astype(f32)

            def build_carry(g, carry):
                block_rows = pl.ds(pl.multiple_of(g * BLOCK, BLOCK), BLOCK)
                value = weight_wide[pl.ds(g, 1), :] * jnp.exp(-decay_wide[pl.ds(g, 1), :] * ahead)
                high = value.astype(bf16).astype(f32)
                carry_taps[block_rows, 0:BLOCK] = jnp.where(
                    lane_index < 2 * mode_count, high, value - high
                ).astype(bf16)
                row = medium_rev[1, pl.ds(spot * group_count + g, 1), :]
                rolled = pltpu.roll(
                    jnp.broadcast_to(row, (BLOCK, BLOCK)), 0, 1, stride=1, stride_axis=0
                )
                carry_taps[block_rows, BLOCK : 2 * BLOCK] = jnp.where(upper, rolled, 0.0).astype(
                    bf16
                )
                return carry

            lax.fori_loop(0, group_count, build_carry, 0)

    @pl.when(mine == parts - 1)
    def _():
        for place in range(part):
            wait_product(place)

    lane_group = lax.broadcasted_iota(jnp.int32, (BLOCK, 128), 1) // group_width

    def grouped(taps, columns, source, base):
        sums = [jnp.zeros((BLOCK, 128), f32)] * 2
        for first in range(0, tile_groups, 4):
            start = pl.multiple_of(base + first * BLOCK, BLOCK)
            result = jnp.dot(
                taps[pl.ds(start, 4 * BLOCK), columns], source, preferred_element_type=f32
            )
            for g in range(4):
                for side in range(2):
                    sums[side] = jnp.where(
                        lane_group == first + g,
                        result[g * BLOCK : (g + 1) * BLOCK, side * 128 : (side + 1) * 128],
                        sums[side],
                    )
        return sums

    def own_part(tile, carry):
        place = pl.ds(pl.multiple_of(tile * 128, 128), 128)
        base = tile * tile_groups * BLOCK
        for pair in range(pair_count):
            depth = (pair + 1) * 2 * BLOCK
            columns = slice(block_count * BLOCK - depth, block_count * BLOCK)
            source = jnp.concatenate(
                [prod_all[0:depth, place], prod_all[BLOCK : BLOCK + depth, place]], 1
            )
            sums = grouped(toep, columns, source, base)
            for side in range(2):
                at = (pair * 2 + side) * BLOCK
                mixed_sum[at : at + BLOCK, place] = sums[side]
        return carry

    lax.fori_loop(0, tile_count, own_part, 0)

    def mixed_copy(place):
        return pltpu.make_async_remote_copy(
            src_ref=mixed_out.at[place],
            dst_ref=mixed_in.at[spot],
            send_sem=mixed_send.at[place],
            recv_sem=mixed_recv.at[lax.rem(place - spot + part, part)],
            device_id={"ctx": mine * part + place},
            device_id_type=MESH,
        )

    if parts > 1:

        @pl.when(mine > 0)
        def _():
            rim_copy.wait_recv()
            if parts > 2:

                @pl.when(mine == parts - 1)
                def _():
                    state_copy.wait_recv()

            else:
                state_copy.wait_recv()

            for tile in range(tile_count):
                place = slice(tile * 128, (tile + 1) * 128)
                fade = channel_decay(tile)
                carry_rows[0, BLOCK : 2 * BLOCK, tile * 256 : tile * 256 + 128] = rim_in[:, place]
                for block in range(block_count):
                    state = state_in[:, place] * jnp.exp(-fade * (block * BLOCK))
                    high = state.astype(bf16)
                    low = (state - high.astype(f32)).astype(bf16)
                    at = tile * 256 + block % 2 * 128
                    carry_rows[block // 2, 0 : 3 * mode_count, at : at + 128] = jnp.concatenate(
                        [high, low, high], 0
                    )

    pair_spots = 2 * BLOCK // rows
    for pair in range(pair_count):
        if parts > 1:

            @pl.when(mine > 0)
            def _():
                depth = 2 * BLOCK if pair == 0 else BLOCK

                def carried(tile, carry):
                    place = pl.ds(pl.multiple_of(tile * 128, 128), 128)
                    source = carry_rows[
                        pair, 0:depth, pl.ds(pl.multiple_of(tile * 256, 256), 256)
                    ]
                    sums = grouped(
                        carry_taps, slice(0, depth), source, tile * tile_groups * BLOCK
                    )
                    for side in range(2):
                        at = (pair * 2 + side) * BLOCK
                        mixed_sum[at : at + BLOCK, place] += sums[side]
                    return carry

                lax.fori_loop(0, tile_count, carried, 0)

        for place in range(pair * pair_spots, (pair + 1) * pair_spots):
            mixed_out[place] = mixed_sum[place * rows : (place + 1) * rows, :].astype(bf16)

            @pl.when(spot != place)
            def _():
                mixed_copy(place).start()

            @pl.when(spot == place)
            def _():
                mixed_in[place] = mixed_out[place]

    loads[7].wait()
    loads[8].wait()

    def gather_hidden(k, square):
        source = lax.rem(spot - k + part, part)

        @pl.when(k > 0)
        def _():
            pltpu.make_async_remote_copy(
                src_ref=mixed_out.at[0],
                dst_ref=mixed_in.at[source],
                send_sem=mixed_send.at[0],
                recv_sem=mixed_recv.at[k],
                device_id=peer(1),
                device_id_type=MESH,
            ).wait_recv()

        for piece in range(per_spot):
            inside = slice(piece * step, (piece + 1) * step)
            chunk = pl.ds(pl.multiple_of(source * width + piece * step, step), step)
            value = residual_ref[:, chunk].astype(f32) + hidden[:, chunk] * mixed_in[
                source, :, inside
            ].astype(f32)
            hidden[:, chunk] = value
            for tile in range(step // 128):
                cut = value[:, tile * 128 : (tile + 1) * 128]
                square = square + cut * cut
        return square

    square = lax.fori_loop(0, part, gather_hidden, jnp.zeros((rows, 128), f32))
    sq_out[...] = square

    def square_copy(k):
        return pltpu.make_async_remote_copy(
            src_ref=sq_out,
            dst_ref=sq_in.at[k],
            send_sem=sq_send.at[k],
            recv_sem=sq_recv.at[k],
            device_id={"tp": lax.rem(tp_me + k, tpn)},
            device_id_type=MESH,
        )

    for k in range(1, tpn):
        square_copy(k).start()
    for k in range(1, tpn):
        square_copy(k).wait_recv()
        square = square + sq_in[k]
    square_sum = jnp.sum(square, axis=1, keepdims=True)
    scale = 1.0 / jnp.sqrt(square_sum / (channels * tpn) + 1e-05)

    def finish(chunk, carry):
        start = pl.multiple_of(chunk * 256, 256)
        gain = gain_ref[pl.ds(start, 256)].astype(f32).reshape(1, 256)
        place = pl.ds(start, 256)
        out_ref[:, place] = (hidden[:, place] * gain * scale).astype(bf16)
        return carry

    lax.fori_loop(0, channels // 256, finish, 0)

    @pl.when(me < n - 1)
    def _():
        for copy in halo_copies:
            copy.wait_send()

    if parts > 1:

        @pl.when(mine < parts - 1)
        def _():
            rim_copy.wait_send()
            state_copy.wait_send()

    for k in range(1, part):
        product_copy(k).wait_send()
    for place in range(part):

        @pl.when(spot != place)
        def _():
            mixed_copy(place).wait_send()

    for k in range(1, tpn):
        square_copy(k).wait_send()


def fused(part, n, tpn, *args):
    outer_input, inner_input, value_input, taps, medium, decay, residues, residual, gain = args
    rows, channels = outer_input.shape
    width = channels // part
    all_groups, mode_count = decay.shape
    group_count = all_groups // part
    tokens = part * rows
    blocks = tokens // BLOCK
    step = 128
    bf16, f32 = jnp.bfloat16, jnp.float32
    dma = pltpu.SemaphoreType.DMA
    return pl.pallas_call(
        functools.partial(fused_kernel, part, n, tpn),
        out_shape=jax.ShapeDtypeStruct((rows, channels), bf16),
        in_specs=[pl.BlockSpec(memory_space=pltpu.HBM)] * 9,
        out_specs=pl.BlockSpec(memory_space=pltpu.VMEM),
        scratch_shapes=[
            pltpu.VMEM((rows, channels), bf16),
            pltpu.VMEM((rows, channels), bf16),
            pltpu.VMEM((rows, channels), bf16),
            pltpu.VMEM(taps.shape, bf16),
            pltpu.VMEM(medium.shape, bf16),
            pltpu.VMEM((mode_count, all_groups), f32),
            pltpu.VMEM((mode_count, all_groups), f32),
            pltpu.VMEM((rows, channels), bf16),
            pltpu.VMEM(gain.shape, bf16),
            pltpu.VMEM((all_groups, mode_count), f32),
            pltpu.VMEM((all_groups, mode_count), f32),
            pltpu.VMEM((16, channels), bf16),
            pltpu.VMEM((16, channels), bf16),
            pltpu.VMEM((16, channels // 2), bf16),
            pltpu.VMEM((16, channels // 2), bf16),
            pltpu.VMEM((rows + 8, step), f32),
            pltpu.VMEM((rows + 8, step), f32),
            pltpu.VMEM((part, rows, width), bf16),
            pltpu.VMEM((BLOCK + tokens, width), bf16),
            pltpu.VMEM((2, all_groups, BLOCK), f32),
            pltpu.VMEM((blocks + 1, group_count, BLOCK), f32),
            pltpu.VMEM((group_count * BLOCK, tokens), bf16),
            pltpu.VMEM((group_count, 128), f32),
            pltpu.VMEM((group_count, 128), f32),
            pltpu.VMEM((group_count * BLOCK, 2 * BLOCK), bf16),
            pltpu.VMEM((blocks // 2, 2 * BLOCK, 2 * width), bf16),
            pltpu.VMEM((2, group_count * mode_count, tokens), bf16),
            pltpu.VMEM((mode_count, width), f32),
            pltpu.VMEM((mode_count, width), f32),
            pltpu.VMEM((BLOCK, width), bf16),
            pltpu.VMEM((tokens, width), f32),
            pltpu.VMEM((part, rows, width), bf16),
            pltpu.VMEM((part, rows, width), bf16),
            pltpu.VMEM((rows, channels), f32),
            pltpu.VMEM((rows, 128), f32),
            pltpu.VMEM((tpn, rows, 128), f32),
            dma((9,)),
            dma((2,)),
            dma((2,)),
            dma((part,)),
            dma((part,)),
            dma((part,)),
            dma((part,)),
            dma((2,)),
            dma((2,)),
            dma((tpn,)),
            dma((tpn,)),
        ],
        compiler_params=pltpu.CompilerParams(
            collective_id=0, has_side_effects=True, vmem_limit_bytes=54200 * 1024
        ),
    )(outer_input, inner_input, value_input, taps, medium, decay.T, residues.T, residual, gain)


PART = 8


def on_device(*args):
    n, tpn = lax.axis_size("ctx"), lax.axis_size("tp")
    rows, channels = args[0].shape
    taps_rows, medium_rows = args[3].shape[1], args[4].shape[0]
    groups, modes = args[5].shape
    fits = (
        n % PART == 0
        and channels % (PART * 128) == 0
        and channels % 1024 == 0
        and BLOCK % rows == 0
        and rows % 32 == 0
        and (PART * rows) % (2 * BLOCK) == 0
        and groups % (8 * PART) == 0
        and 128 % (channels // groups) == 0
        and channels // groups <= 32
        and modes % 16 == 0
        and modes <= 32
        and taps_rows <= 9
        and medium_rows == BLOCK
    )
    if fits:
        return fused(PART, n, tpn, *args)
    return plain(*args)


def solution(mesh):
    return jax.shard_map(
        on_device,
        mesh=mesh,
        in_specs=(
            P("ctx", "tp"),
            P("ctx", "tp"),
            P("ctx", "tp"),
            P(None, None, "tp"),
            P(None, "tp"),
            P("tp", None),
            P("tp", None),
            P("ctx", "tp"),
            P("tp"),
        ),
        out_specs=P("ctx", "tp"),
        check_vma=False,
    )
```

```python
import functools
import jax
import jax.numpy as jnp
from jax import lax
from jax.experimental import pallas as pl
from jax.experimental.pallas import tpu as pltpu
from jax.sharding import PartitionSpec as P

MESH = pl.DeviceIdType.MESH
BLOCK = 128

D = 8192


def passed_along(array, axis, by):
    size = lax.axis_size(axis)
    pairs = [(i, i + by) for i in range(size) if 0 <= i + by < size]
    return lax.ppermute(array, axis, pairs)


def entering(part, axis, combine, identity):
    place = lax.axis_index(axis)
    gathered = jax.tree.map(lambda a: lax.all_gather(a, axis), part)
    state = jax.tree.map(lambda a, e: jnp.zeros_like(a) + jnp.asarray(e, a.dtype), part, identity)

    def one(lap, state):
        return combine(
            state, jax.tree.map(lambda a: lax.dynamic_index_in_dim(a, lap, 0, False), gathered)
        )

    return lax.fori_loop(0, place, one, state)


def banded(reversed_taps, row_count, width):
    group_count, tap_count = reversed_taps.shape
    period = width + 1
    padded = jnp.pad(reversed_taps, ((0, 0), (0, period - tap_count)))
    tiled = jnp.tile(padded, (1, row_count))
    return tiled[:, : row_count * width].reshape(group_count, row_count, width)


def featurize(extended, tap_table, row_count):
    rim_rows = tap_table.shape[0] - 1
    summed = jnp.zeros((row_count, extended.shape[1]), jnp.float32)
    for offset in range(tap_table.shape[0]):
        window = extended[rim_rows - offset : rim_rows - offset + row_count].astype(jnp.float32)
        summed = summed + tap_table[offset].astype(jnp.float32)[None, :] * window
    return summed


def product_rim(product, rim_depth):
    row_count = product.shape[0]
    pieces = []
    for distance in range(1, (rim_depth - 1) // row_count + 2):
        needed = min(row_count, rim_depth - (distance - 1) * row_count)
        arrived = passed_along(product[row_count - needed :], "ctx", distance)
        pieces = [arrived] + pieces
    return jnp.concatenate(pieces, 0)


def combine_modes(earlier, later):
    return (earlier[0] * later[0], earlier[1] * later[0] + later[1])


def plain(
    outer_input,
    inner_input,
    value_input,
    feature_taps,
    medium_taps,
    decay_rates,
    residues,
    residual,
    norm_gain,
):
    row_count, channels = outer_input.shape
    group_count, mode_count = decay_rates.shape
    group_width = channels // group_count
    feat_rim = feature_taps.shape[1] - 1
    medium_rim = medium_taps.shape[0] - 1
    highest = lax.Precision.HIGHEST
    rim_outer, rim_inner, rim_value = passed_along(
        (
            outer_input[row_count - feat_rim :],
            inner_input[row_count - feat_rim :],
            value_input[row_count - feat_rim :],
        ),
        "ctx",
        1,
    )
    inner_feat = featurize(jnp.concatenate([rim_inner, inner_input], 0), feature_taps[1], row_count)
    value_feat = featurize(jnp.concatenate([rim_value, value_input], 0), feature_taps[2], row_count)
    product = (inner_feat * value_feat).astype(jnp.bfloat16)
    extended = jnp.concatenate([product_rim(product, medium_rim), product], 0)
    outer_feat = featurize(jnp.concatenate([rim_outer, outer_input], 0), feature_taps[0], row_count)
    band_medium = banded(medium_taps[::-1].T, row_count, row_count + medium_rim)
    extended_groups = extended.reshape(row_count + medium_rim, group_count, group_width)
    medium_part = jnp.einsum(
        "gts,sgc->tgc", band_medium, extended_groups, preferred_element_type=jnp.float32
    )
    lag_rows = jnp.arange(row_count, dtype=jnp.float32)[:, None, None]
    mode_weight = residues * jnp.sqrt(2.0 * decay_rates / mode_count)
    powers = jnp.exp(-decay_rates[None] * lag_rows)
    long_taps = jnp.sum(powers * mode_weight[None], axis=2)
    band_long = banded(long_taps[::-1].T, row_count, 2 * row_count - 1)[:, :, row_count - 1 :]
    product_wide = product.reshape(row_count, group_count, group_width).astype(jnp.float32)
    within = jnp.einsum("gts,sgc->tgc", band_long, product_wide, precision=highest)
    to_end = jnp.exp(-decay_rates[None] * (row_count - 1.0 - lag_rows))
    local_state = jnp.einsum("tgc,tgn->gcn", product_wide, to_end, precision=highest)
    block_decay = jnp.exp(-decay_rates * row_count)[:, None, :]
    neutral = (jnp.ones_like(block_decay), jnp.zeros_like(local_state))
    prefix = entering((block_decay, local_state), "ctx", combine_modes, neutral)
    incoming = prefix[1]
    from_start = powers * jnp.exp(-decay_rates)[None]
    carried = jnp.einsum(
        "tgn,gcn->tgc", from_start, incoming * mode_weight[:, None, :], precision=highest
    )
    mixed_conv = (medium_part + within + carried).reshape(row_count, channels)
    hidden = residual.astype(jnp.float32) + outer_feat * mixed_conv
    square_sum = lax.psum(jnp.sum(hidden * hidden, axis=1), "tp")
    normed = (
        hidden * norm_gain.astype(jnp.float32)[None, :] / jnp.sqrt(square_sum / D + 1e-05)[:, None]
    ).astype(jnp.bfloat16)
    return normed


def fused_kernel(
    part,
    n,
    tpn,
    outer_hbm,
    inner_hbm,
    value_hbm,
    taps_hbm,
    medium_hbm,
    decay_hbm,
    residues_hbm,
    residual_hbm,
    gain_hbm,
    out_hbm,
    out_ref,
    outer_ref,
    inner_ref,
    value_ref,
    taps_ref,
    medium_ref,
    decay_ref,
    residues_ref,
    residual_ref,
    gain_ref,
    decay_rows,
    weight_rows,
    halo_out,
    halo_in,
    gate_out,
    gate_in,
    ext_a,
    ext_b,
    prod_out,
    prod_all,
    medium_rev,
    filt_rev,
    toep,
    decay_wide,
    weight_wide,
    carry_taps,
    carry_rows,
    state_taps,
    state_out,
    state_in,
    rim_in,
    mixed_sum,
    mixed_out,
    mixed_in,
    hidden,
    sq_out,
    sq_in,
    load_sem,
    store_sem,
    halo_send,
    halo_recv,
    prod_send,
    prod_recv,
    mixed_send,
    mixed_recv,
    link_send,
    link_recv,
    sq_send,
    sq_recv,
):
    f32, bf16 = jnp.float32, jnp.bfloat16
    me = lax.axis_index("ctx")
    tp_me = lax.axis_index("tp")
    parts = n // part
    mine = me // part
    spot = lax.rem(me, part)
    rows, channels = outer_ref.shape
    width = channels // part
    mode_count, all_groups = decay_ref.shape
    group_width = channels // all_groups
    group_count = width // group_width
    tap_count = taps_ref.shape[1]
    tokens = part * rows
    block_count = tokens // BLOCK
    pair_count = block_count // 2
    tile_groups = 128 // group_width
    tile_count = width // 128
    half = channels // 2
    step = 128

    loads = [
        pltpu.make_async_copy(source, target, load_sem.at[index])
        for index, (source, target) in enumerate(
            [
                (inner_hbm, inner_ref),
                (value_hbm, value_ref),
                (outer_hbm, outer_ref),
                (taps_hbm, taps_ref),
                (decay_hbm, decay_ref),
                (residues_hbm, residues_ref),
                (medium_hbm, medium_ref),
                (residual_hbm, residual_ref),
                (gain_hbm, gain_ref),
            ]
        )
    ]
    for load in loads:
        load.start()

    def peer(k):
        return {"ctx": mine * part + lax.rem(spot + k, part)}

    barrier = pltpu.get_barrier_semaphore()

    def signal(device):
        pl.semaphore_signal(barrier, inc=1, device_id=device, device_id_type=MESH)

    for k in range(1, part):
        signal(peer(k))
    for k in range(1, tpn):
        signal({"tp": lax.rem(tp_me + k, tpn)})
    if parts > 1:

        @pl.when(mine > 0)
        def _():
            signal({"ctx": lax.rem(me - part + n, n)})

            @pl.when(spot == 0)
            def _():
                signal({"ctx": lax.rem(me - 1 + n, n)})

    def last_rows(ref, start, size):
        return ref[rows - 16 : rows, pl.ds(start, size)].astype(f32)[8:16]

    for load in loads[:3]:
        load.wait()
    for start in range(0, channels, 512):
        halo_out[:, pl.ds(start, 512)] = jnp.concatenate(
            [last_rows(inner_ref, start, 512), last_rows(value_ref, start, 512)], 0
        ).astype(bf16)
    for start in range(0, half, 512):
        gate_out[:, pl.ds(start, 512)] = jnp.concatenate(
            [last_rows(outer_ref, start, 512), last_rows(outer_ref, half + start, 512)], 0
        ).astype(bf16)

    awaited = part - 1 + tpn - 1
    if parts > 1:
        awaited = awaited + (1 - mine // (parts - 1)) * (1 + (spot + 1) // part)
    pl.semaphore_wait(barrier, awaited)

    def halo_copy(src, dst, index):
        return pltpu.make_async_remote_copy(
            src_ref=src,
            dst_ref=dst,
            send_sem=halo_send.at[index],
            recv_sem=halo_recv.at[index],
            device_id={"ctx": lax.rem(me + 1, n)},
            device_id_type=MESH,
        )

    halo_copies = [halo_copy(halo_out, halo_in, 0), halo_copy(gate_out, gate_in, 1)]

    @pl.when(me < n - 1)
    def _():
        halo_copies[0].start()
        halo_copies[1].start()

    @pl.when(me == 0)
    def _():
        halo_in[...] = jnp.zeros_like(halo_in)
        gate_in[...] = jnp.zeros_like(gate_in)

    loads[3].wait()

    def windows(which, ext, start, size, first, count):
        taps = taps_ref[which, :, pl.ds(start, size)].astype(f32)
        summed = taps[0:1] * ext[first : first + count, :]
        for offset in range(1, tap_count):
            summed = summed + taps[offset : offset + 1] * ext[
                first - offset : first - offset + count, :
            ]
        return summed

    per_spot = width // step

    def lower_product(chunk, carry):
        start = pl.multiple_of(chunk * step, step)
        inside = pl.ds(pl.multiple_of(lax.rem(chunk, per_spot) * step, step), step)
        ext_a[8 : 8 + rows, :] = inner_ref[:, pl.ds(start, step)].astype(f32)
        ext_b[8 : 8 + rows, :] = value_ref[:, pl.ds(start, step)].astype(f32)
        inner_feat = windows(1, ext_a, start, step, 24, rows - 16)
        value_feat = windows(2, ext_b, start, step, 24, rows - 16)
        prod_out[chunk // per_spot, 16:rows, inside] = (inner_feat * value_feat).astype(bf16)
        return carry

    lax.fori_loop(0, channels // step, lower_product, 0, unroll=4)

    @pl.when(me > 0)
    def _():
        halo_copies[0].wait_recv()

    def upper_product(owner):
        for piece in range(per_spot):
            start = pl.multiple_of(owner * width + piece * step, step)
            rim = halo_in[:, pl.ds(start, step)].astype(f32)
            ext_a[0:8, :] = rim[0:8]
            ext_b[0:8, :] = rim[8:16]
            ext_a[8:24, :] = inner_ref[0:16, pl.ds(start, step)].astype(f32)
            ext_b[8:24, :] = value_ref[0:16, pl.ds(start, step)].astype(f32)
            inner_feat = windows(1, ext_a, start, step, 8, 16)
            value_feat = windows(2, ext_b, start, step, 8, 16)
            prod_out[owner, 0:16, piece * step : (piece + 1) * step] = (
                inner_feat * value_feat
            ).astype(bf16)

    def own_rows(place):
        return pl.ds(pl.multiple_of(BLOCK + place * rows, rows), rows)

    def product_copy(k):
        return pltpu.make_async_remote_copy(
            src_ref=prod_out.at[lax.rem(spot + k, part)],
            dst_ref=prod_all.at[own_rows(spot)],
            send_sem=prod_send.at[k],
            recv_sem=prod_recv.at[k],
            device_id=peer(k),
            device_id_type=MESH,
        )

    def send_product(k, carry):
        upper_product(lax.rem(spot + k, part))
        product_copy(k).start()
        return carry

    lax.fori_loop(1, part, send_product, 0)
    upper_product(spot)
    prod_all[own_rows(spot), :] = prod_out[spot]
    prod_all[0:BLOCK, :] = jnp.zeros((BLOCK, width), bf16)

    for load in loads[4:7]:
        load.wait()

    tap_index = lax.broadcasted_iota(jnp.int32, (BLOCK, BLOCK), 0)
    lane_index = lax.broadcasted_iota(jnp.int32, (BLOCK, BLOCK), 1)
    for m in range(2):
        pick = jnp.where(tap_index == BLOCK * m - lane_index, 1.0, 0.0).astype(bf16)
        medium_rev[m] = lax.dot_general(
            medium_ref[...], pick, (((0,), (0,)), ((), ())), preferred_element_type=f32
        )
    own_groups = pl.ds(pl.multiple_of(spot * group_count, group_count), group_count)
    decay_rows[...] = decay_ref[...].T
    weight_rows[...] = (residues_ref[...] * jnp.sqrt(2.0 * decay_ref[...] / mode_count)).T
    decay = decay_rows[own_groups, :]
    weight = weight_rows[own_groups, :]
    lanes = lax.broadcasted_iota(jnp.int32, (group_count, BLOCK), 1)
    for m in range(block_count + 1):
        lag = BLOCK * m - lanes
        lag_rows = jnp.maximum(lag, 0).astype(f32)
        total = jnp.zeros((group_count, BLOCK), f32)
        for mode in range(mode_count):
            total = total + weight[:, mode : mode + 1] * jnp.exp(
                -decay[:, mode : mode + 1] * lag_rows
            )
        total = jnp.where(lag >= 0, total, 0.0)
        if m < 2:
            total = total + medium_rev[m, own_groups, :]
        filt_rev[m] = total

    blank = jnp.zeros((group_count, 128 - 3 * mode_count), f32)
    decay_wide[...] = jnp.concatenate([decay, decay, decay, blank], 1)
    weight_wide[...] = jnp.concatenate([weight, weight, weight, blank], 1)

    mode_row = lax.broadcasted_iota(jnp.int32, (mode_count, 128), 0)
    mode_lane = lax.broadcasted_iota(jnp.int32, (mode_count, 128), 1)

    def decay_column(g):
        row = jnp.broadcast_to(decay_wide[pl.ds(g, 1), :], (mode_count, 128))
        return jnp.sum(jnp.where(mode_row == mode_lane, row, 0.0), axis=1, keepdims=True)

    def channel_decay(tile):
        spread = jnp.zeros((mode_count, 128), f32)
        for g in range(tile_groups):
            spread = jnp.where(
                mode_lane // group_width == g, decay_column(tile * tile_groups + g), spread
            )
        return spread

    if parts > 1:

        @pl.when(mine < parts - 1)
        def _():
            left = (
                tokens - 1 - lax.broadcasted_iota(jnp.int32, (mode_count, tokens), 1)
            ).astype(f32)

            def decays(g, carry):
                place = pl.ds(pl.multiple_of(g * mode_count, mode_count), mode_count)
                value = jnp.exp(-decay_column(g) * left)
                high = value.astype(bf16)
                state_taps[0, place, :] = high
                state_taps[1, place, :] = (value - high.astype(f32)).astype(bf16)
                return carry

            lax.fori_loop(0, group_count, decays, 0)

    @pl.when(me > 0)
    def _():
        halo_copies[1].wait_recv()

    def gate_chunk(chunk, carry):
        start = pl.multiple_of(chunk * step, step)
        low = start < half
        rim_start = pl.multiple_of(lax.rem(start, half), step)
        rim = gate_in[:, pl.ds(rim_start, step)].astype(f32)
        ext_a[0:8, :] = jnp.where(low, rim[0:8], rim[8:16])
        ext_a[8 : 8 + rows, :] = outer_ref[:, pl.ds(start, step)].astype(f32)
        hidden[:, pl.ds(start, step)] = windows(0, ext_a, start, step, 8, rows)
        return carry

    lax.fori_loop(0, channels // step, gate_chunk, 0, unroll=4)

    def wait_product(place):
        @pl.when(spot != place)
        def _():
            pltpu.make_async_remote_copy(
                src_ref=prod_out.at[0],
                dst_ref=prod_all.at[BLOCK + place * rows : BLOCK + (place + 1) * rows],
                send_sem=prod_send.at[0],
                recv_sem=prod_recv.at[lax.rem(spot - place + part, part)],
                device_id=peer(1),
                device_id_type=MESH,
            ).wait_recv()

    def link_copy(src, dst, index):
        return pltpu.make_async_remote_copy(
            src_ref=src,
            dst_ref=dst,
            send_sem=link_send.at[index],
            recv_sem=link_recv.at[index],
            device_id={"ctx": lax.rem(me + part, n)},
            device_id_type=MESH,
        )

    rim_copy = link_copy(prod_all.at[tokens : tokens + BLOCK], rim_in, 0)
    state_copy = link_copy(state_out, state_in, 1)
    rim_spots = part - BLOCK // rows

    if parts > 1:

        @pl.when(mine < parts - 1)
        def _():
            for place in range(rim_spots, part):
                wait_product(place)
            rim_copy.start()
            for place in range(rim_spots):
                wait_product(place)
            tile_rows = tile_groups * mode_count
            for tile in range(tile_count):
                place = slice(tile * 128, (tile + 1) * 128)
                source = prod_all[BLOCK : BLOCK + tokens, place]
                taps_rows = slice(tile * tile_rows, (tile + 1) * tile_rows)
                sums = jnp.dot(
                    state_taps[0, taps_rows, :], source, preferred_element_type=f32
                ) + jnp.dot(state_taps[1, taps_rows, :], source, preferred_element_type=f32)
                state = jnp.zeros((mode_count, 128), f32)
                for g in range(tile_groups):
                    state = jnp.where(
                        mode_lane // group_width == g,
                        sums[g * mode_count : (g + 1) * mode_count],
                        state,
                    )
                state_out[:, place] = state
            if parts > 2:

                @pl.when(mine > 0)
                def _():
                    state_copy.wait_recv()
                    for tile in range(tile_count):
                        place = slice(tile * 128, (tile + 1) * 128)
                        state_out[:, place] = state_out[:, place] + state_in[:, place] * jnp.exp(
                            -channel_decay(tile) * tokens
                        )

            state_copy.start()

    upper = lane_index >= tap_index

    def build(g, carry):
        block_rows = pl.ds(pl.multiple_of(g * BLOCK, BLOCK), BLOCK)
        earlier = None
        for m in range(block_count + 1):
            row = jnp.broadcast_to(filt_rev[m, pl.ds(g, 1), :], (BLOCK, BLOCK))
            rolled = pltpu.roll(row, 0, 1, stride=1, stride_axis=0)
            if m > 0:
                place = (block_count - m) * BLOCK
                toep[block_rows, place : place + BLOCK] = jnp.where(
                    upper, earlier, rolled
                ).astype(bf16)
            earlier = rolled
        return carry

    lax.fori_loop(0, group_count, build, 0, unroll=2)

    if parts > 1:

        @pl.when(mine > 0)
        def _():
            carry_rows[...] = jnp.zeros_like(carry_rows)
            ahead = (tap_index + 1).astype(f32)

            def build_carry(g, carry):
                block_rows = pl.ds(pl.multiple_of(g * BLOCK, BLOCK), BLOCK)
                value = weight_wide[pl.ds(g, 1), :] * jnp.exp(-decay_wide[pl.ds(g, 1), :] * ahead)
                high = value.astype(bf16).astype(f32)
                carry_taps[block_rows, 0:BLOCK] = jnp.where(
                    lane_index < 2 * mode_count, high, value - high
                ).astype(bf16)
                row = medium_rev[1, pl.ds(spot * group_count + g, 1), :]
                rolled = pltpu.roll(
                    jnp.broadcast_to(row, (BLOCK, BLOCK)), 0, 1, stride=1, stride_axis=0
                )
                carry_taps[block_rows, BLOCK : 2 * BLOCK] = jnp.where(upper, rolled, 0.0).astype(
                    bf16
                )
                return carry

            lax.fori_loop(0, group_count, build_carry, 0, unroll=2)

    @pl.when(mine == parts - 1)
    def _():
        for place in range(part):
            wait_product(place)

    lane_group = lax.broadcasted_iota(jnp.int32, (BLOCK, 128), 1) // group_width

    def grouped(taps, columns, source, base):
        sums = [jnp.zeros((BLOCK, 128), f32)] * 2
        for first in range(0, tile_groups, 4):
            start = pl.multiple_of(base + first * BLOCK, BLOCK)
            result = jnp.dot(
                taps[pl.ds(start, 4 * BLOCK), columns], source, preferred_element_type=f32
            )
            for g in range(4):
                for side in range(2):
                    sums[side] = jnp.where(
                        lane_group == first + g,
                        result[g * BLOCK : (g + 1) * BLOCK, side * 128 : (side + 1) * 128],
                        sums[side],
                    )
        return sums

    def mixed_copy(place):
        return pltpu.make_async_remote_copy(
            src_ref=mixed_out.at[place],
            dst_ref=mixed_in.at[spot],
            send_sem=mixed_send.at[place],
            recv_sem=mixed_recv.at[lax.rem(place - spot + part, part)],
            device_id={"ctx": mine * part + place},
            device_id_type=MESH,
        )

    def take_carry():
        rim_copy.wait_recv()
        if parts > 2:

            @pl.when(mine == parts - 1)
            def _():
                state_copy.wait_recv()

        else:
            state_copy.wait_recv()

        for tile in range(tile_count):
            place = slice(tile * 128, (tile + 1) * 128)
            fade = channel_decay(tile)
            carry_rows[0, BLOCK : 2 * BLOCK, tile * 256 : tile * 256 + 128] = rim_in[:, place]
            for block in range(block_count):
                state = state_in[:, place] * jnp.exp(-fade * (block * BLOCK))
                high = state.astype(bf16)
                low = (state - high.astype(f32)).astype(bf16)
                at = tile * 256 + block % 2 * 128
                carry_rows[block // 2, 0 : 3 * mode_count, at : at + 128] = jnp.concatenate(
                    [high, low, high], 0
                )

    pair_spots = 2 * BLOCK // rows
    for pair in range(pair_count):
        depth = (pair + 1) * 2 * BLOCK

        def own_part(tile, carry):
            place = pl.ds(pl.multiple_of(tile * 128, 128), 128)
            columns = slice(block_count * BLOCK - depth, block_count * BLOCK)
            source = jnp.concatenate(
                [prod_all[0:depth, place], prod_all[BLOCK : BLOCK + depth, place]], 1
            )
            sums = grouped(toep, columns, source, tile * tile_groups * BLOCK)
            for side in range(2):
                at = (pair * 2 + side) * BLOCK
                mixed_sum[at : at + BLOCK, place] = sums[side]
            return carry

        lax.fori_loop(0, tile_count, own_part, 0)

        if parts > 1:

            @pl.when(mine > 0)
            def _():
                if pair == 0:
                    take_carry()
                reach = 2 * BLOCK if pair == 0 else BLOCK

                def carried(tile, carry):
                    place = pl.ds(pl.multiple_of(tile * 128, 128), 128)
                    source = carry_rows[
                        pair, 0:reach, pl.ds(pl.multiple_of(tile * 256, 256), 256)
                    ]
                    sums = grouped(
                        carry_taps, slice(0, reach), source, tile * tile_groups * BLOCK
                    )
                    for side in range(2):
                        at = (pair * 2 + side) * BLOCK
                        mixed_sum[at : at + BLOCK, place] += sums[side]
                    return carry

                lax.fori_loop(0, tile_count, carried, 0)

        for place in range(pair * pair_spots, (pair + 1) * pair_spots):
            mixed_out[place] = mixed_sum[place * rows : (place + 1) * rows, :].astype(bf16)

            @pl.when(spot != place)
            def _():
                mixed_copy(place).start()

            @pl.when(spot == place)
            def _():
                mixed_in[place] = mixed_out[place]

    loads[7].wait()
    loads[8].wait()

    def gather_hidden(k, square):
        source = lax.rem(spot - k + part, part)

        @pl.when(k > 0)
        def _():
            pltpu.make_async_remote_copy(
                src_ref=mixed_out.at[0],
                dst_ref=mixed_in.at[source],
                send_sem=mixed_send.at[0],
                recv_sem=mixed_recv.at[k],
                device_id=peer(1),
                device_id_type=MESH,
            ).wait_recv()

        for piece in range(per_spot):
            inside = slice(piece * step, (piece + 1) * step)
            chunk = pl.ds(pl.multiple_of(source * width + piece * step, step), step)
            value = residual_ref[:, chunk].astype(f32) + hidden[:, chunk] * mixed_in[
                source, :, inside
            ].astype(f32)
            hidden[:, chunk] = value
            for tile in range(step // 128):
                cut = value[:, tile * 128 : (tile + 1) * 128]
                square = square + cut * cut
        return square

    square = lax.fori_loop(0, part, gather_hidden, jnp.zeros((rows, 128), f32))
    sq_out[...] = square

    def square_copy(k):
        return pltpu.make_async_remote_copy(
            src_ref=sq_out,
            dst_ref=sq_in.at[k],
            send_sem=sq_send.at[k],
            recv_sem=sq_recv.at[k],
            device_id={"tp": lax.rem(tp_me + k, tpn)},
            device_id_type=MESH,
        )

    for k in range(1, tpn):
        square_copy(k).start()
    for k in range(1, tpn):
        square_copy(k).wait_recv()
        square = square + sq_in[k]
    square_sum = jnp.sum(square, axis=1, keepdims=True)
    scale = 1.0 / jnp.sqrt(square_sum / (channels * tpn) + 1e-05)

    quarter = channels // 4
    stores = []
    for part_index in range(4):
        place = slice(part_index * quarter, (part_index + 1) * quarter)
        gain = gain_ref[place].astype(f32).reshape(1, quarter)
        out_ref[:, place] = (hidden[:, place] * gain * scale).astype(bf16)
        stores.append(
            pltpu.make_async_copy(
                out_ref.at[:, place], out_hbm.at[:, place], store_sem.at[part_index]
            )
        )
        stores[-1].start()

    @pl.when(me < n - 1)
    def _():
        for copy in halo_copies:
            copy.wait_send()

    if parts > 1:

        @pl.when(mine < parts - 1)
        def _():
            rim_copy.wait_send()
            state_copy.wait_send()

    for k in range(1, part):
        product_copy(k).wait_send()
    for place in range(part):

        @pl.when(spot != place)
        def _():
            mixed_copy(place).wait_send()

    for k in range(1, tpn):
        square_copy(k).wait_send()
    for store in stores:
        store.wait()


def fused(part, n, tpn, *args):
    outer_input, inner_input, value_input, taps, medium, decay, residues, residual, gain = args
    rows, channels = outer_input.shape
    width = channels // part
    all_groups, mode_count = decay.shape
    group_count = all_groups // part
    tokens = part * rows
    blocks = tokens // BLOCK
    step = 128
    bf16, f32 = jnp.bfloat16, jnp.float32
    dma = pltpu.SemaphoreType.DMA
    return pl.pallas_call(
        functools.partial(fused_kernel, part, n, tpn),
        out_shape=jax.ShapeDtypeStruct((rows, channels), bf16),
        in_specs=[pl.BlockSpec(memory_space=pltpu.HBM)] * 9,
        out_specs=pl.BlockSpec(memory_space=pltpu.HBM),
        scratch_shapes=[
            pltpu.VMEM((rows, channels), bf16),
            pltpu.VMEM((rows, channels), bf16),
            pltpu.VMEM((rows, channels), bf16),
            pltpu.VMEM((rows, channels), bf16),
            pltpu.VMEM(taps.shape, bf16),
            pltpu.VMEM(medium.shape, bf16),
            pltpu.VMEM((mode_count, all_groups), f32),
            pltpu.VMEM((mode_count, all_groups), f32),
            pltpu.VMEM((rows, channels), bf16),
            pltpu.VMEM(gain.shape, bf16),
            pltpu.VMEM((all_groups, mode_count), f32),
            pltpu.VMEM((all_groups, mode_count), f32),
            pltpu.VMEM((16, channels), bf16),
            pltpu.VMEM((16, channels), bf16),
            pltpu.VMEM((16, channels // 2), bf16),
            pltpu.VMEM((16, channels // 2), bf16),
            pltpu.VMEM((rows + 8, step), f32),
            pltpu.VMEM((rows + 8, step), f32),
            pltpu.VMEM((part, rows, width), bf16),
            pltpu.VMEM((BLOCK + tokens, width), bf16),
            pltpu.VMEM((2, all_groups, BLOCK), f32),
            pltpu.VMEM((blocks + 1, group_count, BLOCK), f32),
            pltpu.VMEM((group_count * BLOCK, tokens), bf16),
            pltpu.VMEM((group_count, 128), f32),
            pltpu.VMEM((group_count, 128), f32),
            pltpu.VMEM((group_count * BLOCK, 2 * BLOCK), bf16),
            pltpu.VMEM((blocks // 2, 2 * BLOCK, 2 * width), bf16),
            pltpu.VMEM((2, group_count * mode_count, tokens), bf16),
            pltpu.VMEM((mode_count, width), f32),
            pltpu.VMEM((mode_count, width), f32),
            pltpu.VMEM((BLOCK, width), bf16),
            pltpu.VMEM((tokens, width), f32),
            pltpu.VMEM((part, rows, width), bf16),
            pltpu.VMEM((part, rows, width), bf16),
            pltpu.VMEM((rows, channels), f32),
            pltpu.VMEM((rows, 128), f32),
            pltpu.VMEM((tpn, rows, 128), f32),
            dma((9,)),
            dma((4,)),
            dma((2,)),
            dma((2,)),
            dma((part,)),
            dma((part,)),
            dma((part,)),
            dma((part,)),
            dma((2,)),
            dma((2,)),
            dma((tpn,)),
            dma((tpn,)),
        ],
        compiler_params=pltpu.CompilerParams(
            collective_id=0, has_side_effects=True, vmem_limit_bytes=63 * 1024 * 1024
        ),
    )(outer_input, inner_input, value_input, taps, medium, decay.T, residues.T, residual, gain)


PART = 8


def on_device(*args):
    n, tpn = lax.axis_size("ctx"), lax.axis_size("tp")
    rows, channels = args[0].shape
    taps_rows, medium_rows = args[3].shape[1], args[4].shape[0]
    groups, modes = args[5].shape
    fits = (
        n % PART == 0
        and channels % (PART * 128) == 0
        and channels % 1024 == 0
        and BLOCK % rows == 0
        and rows % 32 == 0
        and (PART * rows) % (2 * BLOCK) == 0
        and groups % (8 * PART) == 0
        and 128 % (channels // groups) == 0
        and channels // groups <= 32
        and modes % 16 == 0
        and modes <= 32
        and taps_rows <= 9
        and medium_rows == BLOCK
    )
    if fits:
        return fused(PART, n, tpn, *args)
    return plain(*args)


def solution(mesh):
    return jax.shard_map(
        on_device,
        mesh=mesh,
        in_specs=(
            P("ctx", "tp"),
            P("ctx", "tp"),
            P("ctx", "tp"),
            P(None, None, "tp"),
            P(None, "tp"),
            P("tp", None),
            P("tp", None),
            P("ctx", "tp"),
            P("tp"),
        ),
        out_specs=P("ctx", "tp"),
        check_vma=False,
    )
```

```python
import functools
import jax
import jax.numpy as jnp
from jax import lax
from jax.experimental import pallas as pl
from jax.experimental.pallas import tpu as pltpu
from jax.sharding import PartitionSpec as P

MESH = pl.DeviceIdType.MESH
BLOCK = 128

D = 8192


def passed_along(array, axis, by):
    size = lax.axis_size(axis)
    pairs = [(i, i + by) for i in range(size) if 0 <= i + by < size]
    return lax.ppermute(array, axis, pairs)


def entering(part, axis, combine, identity):
    place = lax.axis_index(axis)
    gathered = jax.tree.map(lambda a: lax.all_gather(a, axis), part)
    state = jax.tree.map(lambda a, e: jnp.zeros_like(a) + jnp.asarray(e, a.dtype), part, identity)

    def one(lap, state):
        return combine(
            state, jax.tree.map(lambda a: lax.dynamic_index_in_dim(a, lap, 0, False), gathered)
        )

    return lax.fori_loop(0, place, one, state)


def banded(reversed_taps, row_count, width):
    group_count, tap_count = reversed_taps.shape
    period = width + 1
    padded = jnp.pad(reversed_taps, ((0, 0), (0, period - tap_count)))
    tiled = jnp.tile(padded, (1, row_count))
    return tiled[:, : row_count * width].reshape(group_count, row_count, width)


def featurize(extended, tap_table, row_count):
    rim_rows = tap_table.shape[0] - 1
    summed = jnp.zeros((row_count, extended.shape[1]), jnp.float32)
    for offset in range(tap_table.shape[0]):
        window = extended[rim_rows - offset : rim_rows - offset + row_count].astype(jnp.float32)
        summed = summed + tap_table[offset].astype(jnp.float32)[None, :] * window
    return summed


def product_rim(product, rim_depth):
    row_count = product.shape[0]
    pieces = []
    for distance in range(1, (rim_depth - 1) // row_count + 2):
        needed = min(row_count, rim_depth - (distance - 1) * row_count)
        arrived = passed_along(product[row_count - needed :], "ctx", distance)
        pieces = [arrived] + pieces
    return jnp.concatenate(pieces, 0)


def combine_modes(earlier, later):
    return (earlier[0] * later[0], earlier[1] * later[0] + later[1])


def plain(
    outer_input,
    inner_input,
    value_input,
    feature_taps,
    medium_taps,
    decay_rates,
    residues,
    residual,
    norm_gain,
):
    row_count, channels = outer_input.shape
    group_count, mode_count = decay_rates.shape
    group_width = channels // group_count
    feat_rim = feature_taps.shape[1] - 1
    medium_rim = medium_taps.shape[0] - 1
    highest = lax.Precision.HIGHEST
    rim_outer, rim_inner, rim_value = passed_along(
        (
            outer_input[row_count - feat_rim :],
            inner_input[row_count - feat_rim :],
            value_input[row_count - feat_rim :],
        ),
        "ctx",
        1,
    )
    inner_feat = featurize(jnp.concatenate([rim_inner, inner_input], 0), feature_taps[1], row_count)
    value_feat = featurize(jnp.concatenate([rim_value, value_input], 0), feature_taps[2], row_count)
    product = (inner_feat * value_feat).astype(jnp.bfloat16)
    extended = jnp.concatenate([product_rim(product, medium_rim), product], 0)
    outer_feat = featurize(jnp.concatenate([rim_outer, outer_input], 0), feature_taps[0], row_count)
    band_medium = banded(medium_taps[::-1].T, row_count, row_count + medium_rim)
    extended_groups = extended.reshape(row_count + medium_rim, group_count, group_width)
    medium_part = jnp.einsum(
        "gts,sgc->tgc", band_medium, extended_groups, preferred_element_type=jnp.float32
    )
    lag_rows = jnp.arange(row_count, dtype=jnp.float32)[:, None, None]
    mode_weight = residues * jnp.sqrt(2.0 * decay_rates / mode_count)
    powers = jnp.exp(-decay_rates[None] * lag_rows)
    long_taps = jnp.sum(powers * mode_weight[None], axis=2)
    band_long = banded(long_taps[::-1].T, row_count, 2 * row_count - 1)[:, :, row_count - 1 :]
    product_wide = product.reshape(row_count, group_count, group_width).astype(jnp.float32)
    within = jnp.einsum("gts,sgc->tgc", band_long, product_wide, precision=highest)
    to_end = jnp.exp(-decay_rates[None] * (row_count - 1.0 - lag_rows))
    local_state = jnp.einsum("tgc,tgn->gcn", product_wide, to_end, precision=highest)
    block_decay = jnp.exp(-decay_rates * row_count)[:, None, :]
    neutral = (jnp.ones_like(block_decay), jnp.zeros_like(local_state))
    prefix = entering((block_decay, local_state), "ctx", combine_modes, neutral)
    incoming = prefix[1]
    from_start = powers * jnp.exp(-decay_rates)[None]
    carried = jnp.einsum(
        "tgn,gcn->tgc", from_start, incoming * mode_weight[:, None, :], precision=highest
    )
    mixed_conv = (medium_part + within + carried).reshape(row_count, channels)
    hidden = residual.astype(jnp.float32) + outer_feat * mixed_conv
    square_sum = lax.psum(jnp.sum(hidden * hidden, axis=1), "tp")
    normed = (
        hidden * norm_gain.astype(jnp.float32)[None, :] / jnp.sqrt(square_sum / D + 1e-05)[:, None]
    ).astype(jnp.bfloat16)
    return normed


def fused_kernel(
    part,
    n,
    tpn,
    outer_hbm,
    inner_hbm,
    value_hbm,
    taps_hbm,
    medium_hbm,
    decay_hbm,
    residues_hbm,
    residual_hbm,
    gain_hbm,
    out_hbm,
    out_ref,
    outer_ref,
    inner_ref,
    value_ref,
    taps_ref,
    medium_ref,
    decay_ref,
    residues_ref,
    residual_ref,
    gain_ref,
    decay_rows,
    weight_rows,
    halo_out,
    halo_in,
    gate_out,
    gate_in,
    ext_a,
    ext_b,
    prod_out,
    prod_all,
    medium_rev,
    filt_rev,
    toep,
    decay_wide,
    weight_wide,
    carry_taps,
    carry_rows,
    state_taps,
    state_out,
    state_in,
    rim_in,
    mixed_sum,
    mixed_out,
    mixed_in,
    hidden,
    sq_out,
    sq_in,
    load_sem,
    store_sem,
    halo_send,
    halo_recv,
    prod_send,
    prod_recv,
    mixed_send,
    mixed_recv,
    link_send,
    link_recv,
    sq_send,
    sq_recv,
):
    f32, bf16 = jnp.float32, jnp.bfloat16
    me = lax.axis_index("ctx")
    tp_me = lax.axis_index("tp")
    parts = n // part
    mine = me // part
    spot = lax.rem(me, part)
    rows, channels = outer_ref.shape
    width = channels // part
    mode_count, all_groups = decay_ref.shape
    group_width = channels // all_groups
    group_count = width // group_width
    tap_count = taps_ref.shape[1]
    tokens = part * rows
    block_count = tokens // BLOCK
    pair_count = block_count // 2
    tile_groups = 128 // group_width
    tile_count = width // 128
    half = channels // 2
    step = 128

    loads = [
        pltpu.make_async_copy(source, target, load_sem.at[index])
        for index, (source, target) in enumerate(
            [
                (inner_hbm, inner_ref),
                (value_hbm, value_ref),
                (outer_hbm, outer_ref),
                (taps_hbm, taps_ref),
                (decay_hbm, decay_ref),
                (residues_hbm, residues_ref),
                (medium_hbm, medium_ref),
                (residual_hbm, residual_ref),
                (gain_hbm, gain_ref),
            ]
        )
    ]
    for load in loads:
        load.start()

    def peer(k):
        return {"ctx": mine * part + lax.rem(spot + k, part)}

    barrier = pltpu.get_barrier_semaphore()

    def signal(device):
        pl.semaphore_signal(barrier, inc=1, device_id=device, device_id_type=MESH)

    for k in range(1, part):
        signal(peer(k))
    for k in range(1, tpn):
        signal({"tp": lax.rem(tp_me + k, tpn)})
    if parts > 1:

        @pl.when(mine > 0)
        def _():
            signal({"ctx": lax.rem(me - part + n, n)})

            @pl.when(spot == 0)
            def _():
                signal({"ctx": lax.rem(me - 1 + n, n)})

    def last_rows(ref, start, size):
        return ref[rows - 16 : rows, pl.ds(start, size)].astype(f32)[8:16]

    for load in loads[:3]:
        load.wait()
    for start in range(0, channels, 512):
        halo_out[:, pl.ds(start, 512)] = jnp.concatenate(
            [last_rows(inner_ref, start, 512), last_rows(value_ref, start, 512)], 0
        ).astype(bf16)
    for start in range(0, half, 512):
        gate_out[:, pl.ds(start, 512)] = jnp.concatenate(
            [last_rows(outer_ref, start, 512), last_rows(outer_ref, half + start, 512)], 0
        ).astype(bf16)

    awaited = part - 1 + tpn - 1
    if parts > 1:
        awaited = awaited + (1 - mine // (parts - 1)) * (1 + (spot + 1) // part)
    pl.semaphore_wait(barrier, awaited)

    def halo_copy(src, dst, index):
        return pltpu.make_async_remote_copy(
            src_ref=src,
            dst_ref=dst,
            send_sem=halo_send.at[index],
            recv_sem=halo_recv.at[index],
            device_id={"ctx": lax.rem(me + 1, n)},
            device_id_type=MESH,
        )

    halo_copies = [halo_copy(halo_out, halo_in, 0), halo_copy(gate_out, gate_in, 1)]

    @pl.when(me < n - 1)
    def _():
        halo_copies[0].start()
        halo_copies[1].start()

    @pl.when(me == 0)
    def _():
        halo_in[...] = jnp.zeros_like(halo_in)
        gate_in[...] = jnp.zeros_like(gate_in)

    loads[3].wait()

    def windows(which, ext, start, size, first, count):
        taps = taps_ref[which, :, pl.ds(start, size)].astype(f32)
        summed = taps[0:1] * ext[first : first + count, :]
        for offset in range(1, tap_count):
            summed = summed + taps[offset : offset + 1] * ext[
                first - offset : first - offset + count, :
            ]
        return summed

    per_spot = width // step

    def lower_product(owner, carry):
        for piece in range(per_spot):
            low, high = ext_a.at[piece], ext_b.at[piece]
            start = pl.multiple_of(owner * width + piece * step, step)
            low[8 : 8 + rows, :] = inner_ref[:, pl.ds(start, step)].astype(f32)
            high[8 : 8 + rows, :] = value_ref[:, pl.ds(start, step)].astype(f32)
            inner_feat = windows(1, low, start, step, 24, rows - 16)
            value_feat = windows(2, high, start, step, 24, rows - 16)
            prod_out[owner, 16:rows, piece * step : (piece + 1) * step] = (
                inner_feat * value_feat
            ).astype(bf16)
        return carry

    lax.fori_loop(0, part, lower_product, 0)

    @pl.when(me > 0)
    def _():
        halo_copies[0].wait_recv()

    def upper_product(owner):
        for piece in range(per_spot):
            low, high = ext_a.at[piece], ext_b.at[piece]
            start = pl.multiple_of(owner * width + piece * step, step)
            rim = halo_in[:, pl.ds(start, step)].astype(f32)
            low[0:8, :] = rim[0:8]
            high[0:8, :] = rim[8:16]
            low[8:24, :] = inner_ref[0:16, pl.ds(start, step)].astype(f32)
            high[8:24, :] = value_ref[0:16, pl.ds(start, step)].astype(f32)
            inner_feat = windows(1, low, start, step, 8, 16)
            value_feat = windows(2, high, start, step, 8, 16)
            prod_out[owner, 0:16, piece * step : (piece + 1) * step] = (
                inner_feat * value_feat
            ).astype(bf16)

    def own_rows(place):
        return pl.ds(pl.multiple_of(BLOCK + place * rows, rows), rows)

    def product_copy(k):
        return pltpu.make_async_remote_copy(
            src_ref=prod_out.at[lax.rem(spot + k, part)],
            dst_ref=prod_all.at[own_rows(spot)],
            send_sem=prod_send.at[k],
            recv_sem=prod_recv.at[k],
            device_id=peer(k),
            device_id_type=MESH,
        )

    def send_product(k, carry):
        upper_product(lax.rem(spot + k, part))
        product_copy(k).start()
        return carry

    lax.fori_loop(1, part, send_product, 0)
    upper_product(spot)
    prod_all[own_rows(spot), :] = prod_out[spot]
    prod_all[0:BLOCK, :] = jnp.zeros((BLOCK, width), bf16)

    for load in loads[4:7]:
        load.wait()

    tap_index = lax.broadcasted_iota(jnp.int32, (BLOCK, BLOCK), 0)
    lane_index = lax.broadcasted_iota(jnp.int32, (BLOCK, BLOCK), 1)
    for m in range(2):
        pick = jnp.where(tap_index == BLOCK * m - lane_index, 1.0, 0.0).astype(bf16)
        medium_rev[m] = lax.dot_general(
            medium_ref[...], pick, (((0,), (0,)), ((), ())), preferred_element_type=f32
        )
    own_groups = pl.ds(pl.multiple_of(spot * group_count, group_count), group_count)
    decay_rows[...] = decay_ref[...].T
    weight_rows[...] = (residues_ref[...] * jnp.sqrt(2.0 * decay_ref[...] / mode_count)).T
    decay = decay_rows[own_groups, :]
    weight = weight_rows[own_groups, :]
    lanes = lax.broadcasted_iota(jnp.int32, (group_count, BLOCK), 1)
    for m in range(block_count + 1):
        lag = BLOCK * m - lanes
        lag_rows = jnp.maximum(lag, 0).astype(f32)
        total = jnp.zeros((group_count, BLOCK), f32)
        for mode in range(mode_count):
            total = total + weight[:, mode : mode + 1] * jnp.exp(
                -decay[:, mode : mode + 1] * lag_rows
            )
        total = jnp.where(lag >= 0, total, 0.0)
        if m < 2:
            total = total + medium_rev[m, own_groups, :]
        filt_rev[m] = total

    blank = jnp.zeros((group_count, 128 - 3 * mode_count), f32)
    decay_wide[...] = jnp.concatenate([decay, decay, decay, blank], 1)
    weight_wide[...] = jnp.concatenate([weight, weight, weight, blank], 1)

    mode_row = lax.broadcasted_iota(jnp.int32, (mode_count, 128), 0)
    mode_lane = lax.broadcasted_iota(jnp.int32, (mode_count, 128), 1)

    def decay_column(g):
        row = jnp.broadcast_to(decay_wide[pl.ds(g, 1), :], (mode_count, 128))
        return jnp.sum(jnp.where(mode_row == mode_lane, row, 0.0), axis=1, keepdims=True)

    def channel_decay(tile):
        spread = jnp.zeros((mode_count, 128), f32)
        for g in range(tile_groups):
            spread = jnp.where(
                mode_lane // group_width == g, decay_column(tile * tile_groups + g), spread
            )
        return spread

    if parts > 1:

        @pl.when(mine < parts - 1)
        def _():
            left = (
                tokens - 1 - lax.broadcasted_iota(jnp.int32, (mode_count, tokens), 1)
            ).astype(f32)

            def decays(g, carry):
                place = pl.ds(pl.multiple_of(g * mode_count, mode_count), mode_count)
                value = jnp.exp(-decay_column(g) * left)
                high = value.astype(bf16)
                state_taps[0, place, :] = high
                state_taps[1, place, :] = (value - high.astype(f32)).astype(bf16)
                return carry

            lax.fori_loop(0, group_count, decays, 0, unroll=4)

    def wait_product(place):
        @pl.when(spot != place)
        def _():
            pltpu.make_async_remote_copy(
                src_ref=prod_out.at[0],
                dst_ref=prod_all.at[BLOCK + place * rows : BLOCK + (place + 1) * rows],
                send_sem=prod_send.at[0],
                recv_sem=prod_recv.at[lax.rem(spot - place + part, part)],
                device_id=peer(1),
                device_id_type=MESH,
            ).wait_recv()

    def link_copy(src, dst, index):
        return pltpu.make_async_remote_copy(
            src_ref=src,
            dst_ref=dst,
            send_sem=link_send.at[index],
            recv_sem=link_recv.at[index],
            device_id={"ctx": lax.rem(me + part, n)},
            device_id_type=MESH,
        )

    rim_copy = link_copy(prod_all.at[tokens : tokens + BLOCK], rim_in, 0)
    state_copy = link_copy(state_out, state_in, 1)
    rim_spots = part - BLOCK // rows

    if parts > 1:

        @pl.when(mine < parts - 1)
        def _():
            for place in range(rim_spots, part):
                wait_product(place)
            rim_copy.start()
            for place in range(rim_spots):
                wait_product(place)
            tile_rows = tile_groups * mode_count
            for tile in range(tile_count):
                place = slice(tile * 128, (tile + 1) * 128)
                source = prod_all[BLOCK : BLOCK + tokens, place]
                taps_rows = slice(tile * tile_rows, (tile + 1) * tile_rows)
                sums = jnp.dot(
                    state_taps[0, taps_rows, :], source, preferred_element_type=f32
                ) + jnp.dot(state_taps[1, taps_rows, :], source, preferred_element_type=f32)
                state = jnp.zeros((mode_count, 128), f32)
                for g in range(tile_groups):
                    state = jnp.where(
                        mode_lane // group_width == g,
                        sums[g * mode_count : (g + 1) * mode_count],
                        state,
                    )
                state_out[:, place] = state
            if parts > 2:

                @pl.when(mine > 0)
                def _():
                    state_copy.wait_recv()
                    for tile in range(tile_count):
                        place = slice(tile * 128, (tile + 1) * 128)
                        state_out[:, place] = state_out[:, place] + state_in[:, place] * jnp.exp(
                            -channel_decay(tile) * tokens
                        )

            state_copy.start()

    upper = lane_index >= tap_index

    def build(g, carry):
        block_rows = pl.ds(pl.multiple_of(g * BLOCK, BLOCK), BLOCK)
        earlier = None
        for m in range(block_count + 1):
            row = jnp.broadcast_to(filt_rev[m, pl.ds(g, 1), :], (BLOCK, BLOCK))
            rolled = pltpu.roll(row, 0, 1, stride=1, stride_axis=0)
            if m > 0:
                place = (block_count - m) * BLOCK
                toep[block_rows, place : place + BLOCK] = jnp.where(
                    upper, earlier, rolled
                ).astype(bf16)
            earlier = rolled
        return carry

    lax.fori_loop(0, group_count, build, 0, unroll=2)

    if parts > 1:

        @pl.when(mine > 0)
        def _():
            carry_rows[...] = jnp.zeros_like(carry_rows)
            ahead = (tap_index + 1).astype(f32)

            def build_carry(g, carry):
                block_rows = pl.ds(pl.multiple_of(g * BLOCK, BLOCK), BLOCK)
                value = weight_wide[pl.ds(g, 1), :] * jnp.exp(-decay_wide[pl.ds(g, 1), :] * ahead)
                high = value.astype(bf16).astype(f32)
                carry_taps[block_rows, 0:BLOCK] = jnp.where(
                    lane_index < 2 * mode_count, high, value - high
                ).astype(bf16)
                row = medium_rev[1, pl.ds(spot * group_count + g, 1), :]
                rolled = pltpu.roll(
                    jnp.broadcast_to(row, (BLOCK, BLOCK)), 0, 1, stride=1, stride_axis=0
                )
                carry_taps[block_rows, BLOCK : 2 * BLOCK] = jnp.where(upper, rolled, 0.0).astype(
                    bf16
                )
                return carry

            lax.fori_loop(0, group_count, build_carry, 0, unroll=2)

    @pl.when(mine == parts - 1)
    def _():
        for place in range(part):
            wait_product(place)

    lane_group = lax.broadcasted_iota(jnp.int32, (BLOCK, 128), 1) // group_width

    def grouped(taps, columns, source, base):
        sums = [jnp.zeros((BLOCK, 128), f32)] * 2
        for first in range(0, tile_groups, 4):
            start = pl.multiple_of(base + first * BLOCK, BLOCK)
            result = jnp.dot(
                taps[pl.ds(start, 4 * BLOCK), columns], source, preferred_element_type=f32
            )
            for g in range(4):
                for side in range(2):
                    sums[side] = jnp.where(
                        lane_group == first + g,
                        result[g * BLOCK : (g + 1) * BLOCK, side * 128 : (side + 1) * 128],
                        sums[side],
                    )
        return sums

    def mixed_copy(place):
        return pltpu.make_async_remote_copy(
            src_ref=mixed_out.at[place],
            dst_ref=mixed_in.at[spot],
            send_sem=mixed_send.at[place],
            recv_sem=mixed_recv.at[lax.rem(place - spot + part, part)],
            device_id={"ctx": mine * part + place},
            device_id_type=MESH,
        )

    def take_carry():
        rim_copy.wait_recv()
        if parts > 2:

            @pl.when(mine == parts - 1)
            def _():
                state_copy.wait_recv()

        else:
            state_copy.wait_recv()

        for tile in range(tile_count):
            place = slice(tile * 128, (tile + 1) * 128)
            fade = channel_decay(tile)
            carry_rows[0, BLOCK : 2 * BLOCK, tile * 256 : tile * 256 + 128] = rim_in[:, place]
            for block in range(block_count):
                state = state_in[:, place] * jnp.exp(-fade * (block * BLOCK))
                high = state.astype(bf16)
                low = (state - high.astype(f32)).astype(bf16)
                at = tile * 256 + block % 2 * 128
                carry_rows[block // 2, 0 : 3 * mode_count, at : at + 128] = jnp.concatenate(
                    [high, low, high], 0
                )

    pair_spots = 2 * BLOCK // rows
    for pair in range(pair_count):
        depth = (pair + 1) * 2 * BLOCK

        def own_part(tile, carry):
            place = pl.ds(pl.multiple_of(tile * 128, 128), 128)
            columns = slice(block_count * BLOCK - depth, block_count * BLOCK)
            source = jnp.concatenate(
                [prod_all[0:depth, place], prod_all[BLOCK : BLOCK + depth, place]], 1
            )
            sums = grouped(toep, columns, source, tile * tile_groups * BLOCK)
            for side in range(2):
                at = (pair * 2 + side) * BLOCK
                mixed_sum[at : at + BLOCK, place] = sums[side]
            return carry

        lax.fori_loop(0, tile_count, own_part, 0)

        if parts > 1:

            @pl.when(mine > 0)
            def _():
                if pair == 0:
                    take_carry()
                reach = 2 * BLOCK if pair == 0 else BLOCK

                def carried(tile, carry):
                    place = pl.ds(pl.multiple_of(tile * 128, 128), 128)
                    source = carry_rows[
                        pair, 0:reach, pl.ds(pl.multiple_of(tile * 256, 256), 256)
                    ]
                    sums = grouped(
                        carry_taps, slice(0, reach), source, tile * tile_groups * BLOCK
                    )
                    for side in range(2):
                        at = (pair * 2 + side) * BLOCK
                        mixed_sum[at : at + BLOCK, place] += sums[side]
                    return carry

                lax.fori_loop(0, tile_count, carried, 0)

        for place in range(pair * pair_spots, (pair + 1) * pair_spots):
            mixed_out[place] = mixed_sum[place * rows : (place + 1) * rows, :].astype(bf16)

            @pl.when(spot != place)
            def _():
                mixed_copy(place).start()

            @pl.when(spot == place)
            def _():
                mixed_in[place] = mixed_out[place]

    @pl.when(me > 0)
    def _():
        halo_copies[1].wait_recv()

    def gate_chunk(owner, carry):
        low = owner * width < half
        for piece in range(per_spot):
            ext = ext_a.at[piece]
            start = pl.multiple_of(owner * width + piece * step, step)
            rim_start = pl.multiple_of(lax.rem(start, half), step)
            rim = gate_in[:, pl.ds(rim_start, step)].astype(f32)
            ext[0:8, :] = jnp.where(low, rim[0:8], rim[8:16])
            ext[8 : 8 + rows, :] = outer_ref[:, pl.ds(start, step)].astype(f32)
            hidden[:, pl.ds(start, step)] = windows(0, ext, start, step, 8, rows)
        return carry

    lax.fori_loop(0, part, gate_chunk, 0)

    loads[7].wait()
    loads[8].wait()

    def gather_hidden(k, square):
        source = lax.rem(spot - k + part, part)

        @pl.when(k > 0)
        def _():
            pltpu.make_async_remote_copy(
                src_ref=mixed_out.at[0],
                dst_ref=mixed_in.at[source],
                send_sem=mixed_send.at[0],
                recv_sem=mixed_recv.at[k],
                device_id=peer(1),
                device_id_type=MESH,
            ).wait_recv()

        for piece in range(per_spot):
            inside = slice(piece * step, (piece + 1) * step)
            chunk = pl.ds(pl.multiple_of(source * width + piece * step, step), step)
            value = residual_ref[:, chunk].astype(f32) + hidden[:, chunk] * mixed_in[
                source, :, inside
            ].astype(f32)
            hidden[:, chunk] = value
            for tile in range(step // 128):
                cut = value[:, tile * 128 : (tile + 1) * 128]
                square = square + cut * cut
        return square

    square = lax.fori_loop(0, part, gather_hidden, jnp.zeros((rows, 128), f32))
    sq_out[...] = square

    def square_copy(k):
        return pltpu.make_async_remote_copy(
            src_ref=sq_out,
            dst_ref=sq_in.at[k],
            send_sem=sq_send.at[k],
            recv_sem=sq_recv.at[k],
            device_id={"tp": lax.rem(tp_me + k, tpn)},
            device_id_type=MESH,
        )

    for k in range(1, tpn):
        square_copy(k).start()
    for k in range(1, tpn):
        square_copy(k).wait_recv()
        square = square + sq_in[k]
    square_sum = jnp.sum(square, axis=1, keepdims=True)
    scale = 1.0 / jnp.sqrt(square_sum / (channels * tpn) + 1e-05)

    quarter = channels // 4
    stores = []
    for part_index in range(4):
        place = slice(part_index * quarter, (part_index + 1) * quarter)
        gain = gain_ref[place].astype(f32).reshape(1, quarter)
        out_ref[:, place] = (hidden[:, place] * gain * scale).astype(bf16)
        stores.append(
            pltpu.make_async_copy(
                out_ref.at[:, place], out_hbm.at[:, place], store_sem.at[part_index]
            )
        )
        stores[-1].start()

    @pl.when(me < n - 1)
    def _():
        for copy in halo_copies:
            copy.wait_send()

    if parts > 1:

        @pl.when(mine < parts - 1)
        def _():
            rim_copy.wait_send()
            state_copy.wait_send()

    for k in range(1, part):
        product_copy(k).wait_send()
    for place in range(part):

        @pl.when(spot != place)
        def _():
            mixed_copy(place).wait_send()

    for k in range(1, tpn):
        square_copy(k).wait_send()
    for store in stores:
        store.wait()


def fused(part, n, tpn, *args):
    outer_input, inner_input, value_input, taps, medium, decay, residues, residual, gain = args
    rows, channels = outer_input.shape
    width = channels // part
    all_groups, mode_count = decay.shape
    group_count = all_groups // part
    tokens = part * rows
    blocks = tokens // BLOCK
    step = 128
    bf16, f32 = jnp.bfloat16, jnp.float32
    dma = pltpu.SemaphoreType.DMA
    return pl.pallas_call(
        functools.partial(fused_kernel, part, n, tpn),
        out_shape=jax.ShapeDtypeStruct((rows, channels), bf16),
        in_specs=[pl.BlockSpec(memory_space=pltpu.HBM)] * 9,
        out_specs=pl.BlockSpec(memory_space=pltpu.HBM),
        scratch_shapes=[
            pltpu.VMEM((rows, channels), bf16),
            pltpu.VMEM((rows, channels), bf16),
            pltpu.VMEM((rows, channels), bf16),
            pltpu.VMEM((rows, channels), bf16),
            pltpu.VMEM(taps.shape, bf16),
            pltpu.VMEM(medium.shape, bf16),
            pltpu.VMEM((mode_count, all_groups), f32),
            pltpu.VMEM((mode_count, all_groups), f32),
            pltpu.VMEM((rows, channels), bf16),
            pltpu.VMEM(gain.shape, bf16),
            pltpu.VMEM((all_groups, mode_count), f32),
            pltpu.VMEM((all_groups, mode_count), f32),
            pltpu.VMEM((16, channels), bf16),
            pltpu.VMEM((16, channels), bf16),
            pltpu.VMEM((16, channels // 2), bf16),
            pltpu.VMEM((16, channels // 2), bf16),
            pltpu.VMEM((width // step, rows + 8, step), f32),
            pltpu.VMEM((width // step, rows + 8, step), f32),
            pltpu.VMEM((part, rows, width), bf16),
            pltpu.VMEM((BLOCK + tokens, width), bf16),
            pltpu.VMEM((2, all_groups, BLOCK), f32),
            pltpu.VMEM((blocks + 1, group_count, BLOCK), f32),
            pltpu.VMEM((group_count * BLOCK, tokens), bf16),
            pltpu.VMEM((group_count, 128), f32),
            pltpu.VMEM((group_count, 128), f32),
            pltpu.VMEM((group_count * BLOCK, 2 * BLOCK), bf16),
            pltpu.VMEM((blocks // 2, 2 * BLOCK, 2 * width), bf16),
            pltpu.VMEM((2, group_count * mode_count, tokens), bf16),
            pltpu.VMEM((mode_count, width), f32),
            pltpu.VMEM((mode_count, width), f32),
            pltpu.VMEM((BLOCK, width), bf16),
            pltpu.VMEM((tokens, width), f32),
            pltpu.VMEM((part, rows, width), bf16),
            pltpu.VMEM((part, rows, width), bf16),
            pltpu.VMEM((rows, channels), f32),
            pltpu.VMEM((rows, 128), f32),
            pltpu.VMEM((tpn, rows, 128), f32),
            dma((9,)),
            dma((4,)),
            dma((2,)),
            dma((2,)),
            dma((part,)),
            dma((part,)),
            dma((part,)),
            dma((part,)),
            dma((2,)),
            dma((2,)),
            dma((tpn,)),
            dma((tpn,)),
        ],
        compiler_params=pltpu.CompilerParams(
            collective_id=0, has_side_effects=True, vmem_limit_bytes=63 * 1024 * 1024
        ),
    )(outer_input, inner_input, value_input, taps, medium, decay.T, residues.T, residual, gain)


PART = 8


def on_device(*args):
    n, tpn = lax.axis_size("ctx"), lax.axis_size("tp")
    rows, channels = args[0].shape
    taps_rows, medium_rows = args[3].shape[1], args[4].shape[0]
    groups, modes = args[5].shape
    fits = (
        n % PART == 0
        and channels % (PART * 128) == 0
        and channels % 1024 == 0
        and BLOCK % rows == 0
        and rows % 32 == 0
        and (PART * rows) % (2 * BLOCK) == 0
        and groups % (8 * PART) == 0
        and 128 % (channels // groups) == 0
        and channels // groups <= 32
        and modes % 16 == 0
        and modes <= 32
        and taps_rows <= 9
        and medium_rows == BLOCK
    )
    if fits:
        return fused(PART, n, tpn, *args)
    return plain(*args)


def solution(mesh):
    return jax.shard_map(
        on_device,
        mesh=mesh,
        in_specs=(
            P("ctx", "tp"),
            P("ctx", "tp"),
            P("ctx", "tp"),
            P(None, None, "tp"),
            P(None, "tp"),
            P("tp", None),
            P("tp", None),
            P("ctx", "tp"),
            P("tp"),
        ),
        out_specs=P("ctx", "tp"),
        check_vma=False,
    )
```
